512 devices in a mesh: elem: 8 (over z_lo, core), band: 64 (over y, z_hi, x).
Axes of the slice: x: 4, y: 8, z: 8 (z_hi: 2, z_lo: 4; z = z_hi * 4 + z_lo), core: 2. Of those that a mesh axis runs over, the one named last changes fastest.
Arguments:
- coefficients: bfloat16 [32, 128, 8192], P('elem', None, 'band'), may hold values from -6 to 6
- hamiltonian: bfloat16 [32, 27, 128, 128], P('elem'), may hold values from -0.0546875 to 0.0546875
- neighbours: int32 [32, 27], P('elem'), may hold values from 0 to 31, as said below
- basis_values: bfloat16 [32, 4096, 128], P('elem'), may hold values from -0.5 to 0.5
Outputs:
- filtered: bfloat16 [32, 128, 8192], P('elem', None, 'band')
- density: float32 [32, 4096], P('elem', 'band')
The draws below stay inside these ranges and needn't reach their ends.
Inputs may be any that keep to these rules, and one draw needn't show every extreme that they name: `neighbours`: elements sit on a periodic grid of 8 x 2 x 2 cells in an order drawn from the seed; row e lists the elements at offsets (dx, dy, dz) in -1..1, with k = 9 (dx + 1) + 3 (dy + 1) + dz + 1.
All inputs are finite; a program needn't handle non-finite values.
Results may differ from the reference program's by a relative error of at most 0.0065.
Values may be sent and summed in bfloat16 or wider, within the bound.
No kernel may reach another device: no remote copies, remote signals or barrier semaphores. Data moves between devices by JAX's collectives and lax.ppermute only.
A program may use at most 64 MiB of HBM per device.

```python
import jax
import jax.numpy as jnp
from jax import lax

NB = 128
BANDS = 8192
POINTS = 4096
CHEB = 6
ELEMS = 32


def draw_neighbours(key, part):
    mixed = jax.random.fold_in(key, 7919)
    scores = jax.random.randint(mixed, (ELEMS,), 0, 1048576, dtype=jnp.int32)
    scores = scores * ELEMS + jnp.arange(ELEMS, dtype=jnp.int32)
    inverse = jnp.argsort(scores, stable=True).astype(jnp.int32)
    order = jnp.argsort(inverse, stable=True).astype(jnp.int32)
    first = order // 4
    second = order // 2 % 2
    third = order % 2
    offsets = jnp.arange(27, dtype=jnp.int32)
    shift_a = offsets // 9 - 1
    shift_b = offsets // 3 % 3 - 1
    shift_c = offsets % 3 - 1
    span = ELEMS // 4
    near_a = (first[:, None] + shift_a[None, :] + span) % span
    near_b = (second[:, None] + shift_b[None, :] + 2) % 2
    near_c = (third[:, None] + shift_c[None, :] + 2) % 2
    position = near_a * 4 + near_b * 2 + near_c
    return inverse[position].astype(jnp.int32)


def block_levels(rng, shape, cuts, smallest, largest):
    def one(dim, parts):
        draws = jax.random.uniform(jax.random.fold_in(jax.random.fold_in(rng, 6), dim), (parts,), jnp.float32, smallest / len(cuts), largest / len(cuts))
        return jnp.repeat(jnp.exp(draws), shape[dim] // parts).reshape((-1,) + (1,) * (len(shape) - dim - 1))

    gain = one(*cuts[0])
    for cut in cuts[1:]:
        gain = gain * one(*cut)
    return gain


def noise(stream_key, shape, deviation, most, shards=(), kind=jnp.bfloat16):
    factor_of = block_levels(stream_key, shape, shards, -0.22, 0.18) if shards else 1.0
    values = jax.random.normal(stream_key, shape, jnp.float32) * deviation * factor_of
    return jnp.minimum(jnp.maximum(values, -most), most).astype(kind)


def setup_inputs(seed: int = 0) -> dict:
    keys = jax.random.split(jax.random.key(seed), 5)
    return {
        "coefficients": noise(keys[0], (ELEMS, NB, BANDS), 1.0, 6.0, ((0, 8), (2, 64))),
        "hamiltonian": noise(keys[1], (ELEMS, 27, NB, NB), (108 * NB) ** -0.5, 0.0546875, ((0, 8),)),
        "neighbours": draw_neighbours(jax.random.fold_in(keys[4], 71), 0),
        "basis_values": noise(keys[3], (ELEMS, POINTS, NB), NB ** -0.5, 0.5, ((0, 8),)),
    }


def apply_operator(current, hamiltonian, neighbours):
    def one_element(pair):
        block, index = pair
        near = current[index].astype(jnp.float32)
        return jnp.einsum('kij,kjb->ib', block.astype(jnp.float32), near)
    return lax.map(one_element, (hamiltonian, neighbours))


def reference(coefficients, hamiltonian, neighbours, basis_values):
    previous = coefficients.astype(jnp.float32)
    current = apply_operator(coefficients, hamiltonian, neighbours)
    for step in range(CHEB - 1):
        following = 2.0 * apply_operator(current.astype(jnp.bfloat16), hamiltonian, neighbours) - previous
        previous = current
        current = following
    filtered = current.astype(jnp.bfloat16)

    def decode(pair):
        values, coeffs = pair
        orbital = jnp.dot(values, coeffs, preferred_element_type=jnp.float32)
        return jnp.sum(orbital * orbital, axis=1)

    density = lax.map(decode, (basis_values, filtered)) / BANDS
    return filtered, density
```

```python
import functools

import jax
import jax.numpy as jnp
from jax import lax
from jax.experimental import pallas as pl
from jax.experimental.pallas import tpu as pltpu
from jax.sharding import PartitionSpec as P

BANDS = 8192
NB = 128
POINTS = 4096
PLANES = 8
KDIM = 12 * NB
WIDE = 4 * NB
NX = 4
EDGE = 16
BF = jnp.bfloat16
F32 = jnp.float32
NT = (((1,), (1,)), ((), ()))


def fold_kernel(pair_ref, near_ref, h_ref, out_ref):
    e = 2 * pair_ref[0] + pl.program_id(0)
    rows = lax.broadcasted_iota(jnp.int32, (NB, NB), 0)
    cols = lax.broadcasted_iota(jnp.int32, (NB, NB), 1)
    eye = (rows == cols).astype(F32).astype(BF)
    choices = ((1,), (0, 2))
    for dx in range(3):
        ids = [
            near_ref[e, 9 * dx + 3 * b[0] + c[0]] for b in choices for c in choices
        ]
        spot = 0
        for b in choices:
            for c in choices:
                total = None
                for i in b:
                    for j in c:
                        part = lax.dot_general(
                            eye, h_ref[0, 9 * dx + 3 * i + j], NT, preferred_element_type=F32
                        )
                        total = part if total is None else total + part
                rank = jnp.int32(0)
                for other in range(4):
                    if other != spot:
                        rank = rank + (ids[other] < ids[spot]).astype(jnp.int32)
                row = pl.multiple_of((4 * dx + rank) * NB, NB)
                out_ref[0, pl.ds(row, NB), :] = total.astype(BF)
                spot += 1


def fold(hamiltonian, neighbours, pair):
    return pl.pallas_call(
        fold_kernel,
        out_shape=jax.ShapeDtypeStruct((2, KDIM, NB), BF),
        grid_spec=pltpu.PrefetchScalarGridSpec(
            num_scalar_prefetch=2,
            grid=(2,),
            in_specs=[
                pl.BlockSpec((1, 27, NB, NB), lambda t, pair, near: (2 * pair[0] + t, 0, 0, 0))
            ],
            out_specs=pl.BlockSpec((1, KDIM, NB), lambda t, pair, near: (t, 0, 0)),
        ),
        compiler_params=pltpu.CompilerParams(vmem_limit_bytes=16 * 2**20),
        cost_estimate=pl.CostEstimate(flops=2 * 27 * 2 * NB**3, bytes_accessed=2600000, transcendentals=0),
    )(pair, neighbours, hamiltonian)


def turn_kernel(y_ref, near_ref, out_ref):
    for e in range(4):
        block = y_ref[e].astype(F32).T.astype(BF)
        for copy in range(4):
            out_ref[copy, pl.ds(e * NB, NB), :] = block
    for copy in range(4):
        out_ref[copy, pl.ds(4 * NB, EDGE), :] = near_ref[...]


def turn(coefficients, near):
    return pl.pallas_call(
        turn_kernel,
        out_shape=jax.ShapeDtypeStruct((4, 4 * NB + EDGE, NB), BF),
        compiler_params=pltpu.CompilerParams(vmem_limit_bytes=16 * 2**20),
    )(coefficients, near)


def filter_kernel(near_ref, base_ref, *refs):
    h_refs = refs[:16]
    y_own, y_other, b_ref, filt_ref, dens_ref = refs[16:21]
    hbuf, ybuf, za, zb, bbuf, pid, slot, h_sems, b_sem = refs[21:]
    core = base_ref[16]

    rep = jnp.int32(0)
    for x in range(PLANES):
        ids = [near_ref[rep, 9 + 3 * b + c] for b in (1, 0) for c in (1, 0)]
        following = near_ref[rep, 18 + 4]
        for a, b in ((0, 1), (2, 3), (0, 2), (1, 3), (1, 2)):
            ids[a], ids[b] = jnp.minimum(ids[a], ids[b]), jnp.maximum(ids[a], ids[b])
        for r in range(4):
            slot[ids[r]] = 4 * x + r
        rep = following

    def place(g):
        s = slot[g]
        return s // 4, pl.multiple_of((s % 4) * NB, NB), s

    def h_copy(ref, k, g):
        x, lane, s = place(g)
        return pltpu.make_async_copy(
            ref.at[k], hbuf.at[x, :, pl.ds(lane, NB)], h_sems.at[s]
        )

    for i, ref in enumerate(h_refs):
        for k in range(2):
            h_copy(ref, k, base_ref[i] + k).start()
    b_copy = pltpu.make_async_copy(b_ref, bbuf, b_sem)
    b_copy.start()

    for source, side in ((y_own, core), (y_other, 1 - core)):
        for z in range(4):
            for e in range(4):
                x, lane, _ = place((2 * z + side) * 4 + e)
                block = source[z, pl.ds(e * NB, NB), :]
                ybuf[0, x, :, pl.ds(lane, NB)] = block
                za[x, :, pl.ds(lane, NB)] = block.astype(F32)

    def around(src, x):
        return jnp.concatenate(
            [ybuf[src, (x + 7) % 8], ybuf[src, x], ybuf[src, (x + 1) % 8]], axis=1
        )

    for step in range(5):
        src, dst = step % 2, 1 - step % 2
        past = zb if step % 2 == 0 else za
        for x in range(PLANES):
            if step == 0:
                for r in range(4):
                    pltpu.make_async_copy(
                        h_refs[0].at[0], hbuf.at[x, :, pl.ds(r * NB, NB)], h_sems.at[4 * x + r]
                    ).wait()
            acc = jnp.dot(around(src, x), hbuf[x], preferred_element_type=F32)
            new = acc if step == 0 else 2.0 * acc - past[x]
            past[x] = new
            ybuf[dst, x] = new.astype(BF)

    b_copy.wait()
    mine = base_ref[17]
    for e in range(4):
        x, lane, _ = place(mine + e)
        left = lax.rem(x + 7, 8)
        right = lax.rem(x + 1, 8)
        near = jnp.concatenate([ybuf[1, left], ybuf[1, x], ybuf[1, right]], axis=1)
        acc = jnp.dot(near, hbuf[x, :, pl.ds(lane, NB)], preferred_element_type=F32)
        last = (2.0 * acc - za[x, :, pl.ds(lane, NB)]).astype(BF)
        filt_ref[e] = last.astype(F32).T.astype(BF)
        for p in range(0, POINTS, 512):
            phi = lax.dot_general(
                last, bbuf[e, pl.ds(p, 512), :], NT, preferred_element_type=F32
            )
            dens_ref[e : e + 1, p : p + 512] = jnp.sum(phi * phi, axis=0, keepdims=True)


def filtering(near, base, pieces, y_own, y_other, basis_values):
    anywhere = pl.BlockSpec(memory_space=pl.ANY)
    smem = pl.BlockSpec(memory_space=pltpu.SMEM)
    vmem = pl.BlockSpec(memory_space=pltpu.VMEM)
    return pl.pallas_call(
        filter_kernel,
        out_shape=(
            jax.ShapeDtypeStruct((4, NB, NB), BF),
            jax.ShapeDtypeStruct((4, POINTS), F32),
        ),
        in_specs=[smem, smem] + [anywhere] * 16 + [vmem, vmem, anywhere],
        out_specs=(vmem, vmem),
        scratch_shapes=[
            pltpu.VMEM((PLANES, KDIM, WIDE), BF),
            pltpu.VMEM((2, PLANES, NB, WIDE), BF),
            pltpu.VMEM((PLANES, NB, WIDE), F32),
            pltpu.VMEM((PLANES, NB, WIDE), F32),
            pltpu.VMEM((4, POINTS, NB), BF),
            pltpu.SMEM((32,), jnp.int32),
            pltpu.SMEM((32,), jnp.int32),
            pltpu.SemaphoreType.DMA((32,)),
            pltpu.SemaphoreType.DMA,
        ],
        compiler_params=pltpu.CompilerParams(vmem_limit_bytes=48 * 2**20),
    )(near, base, *pieces, y_own, y_other, basis_values)


def routes(nbands):
    def index(y, h, x, lo, core):
        return (lo * 2 + core) * nbands + (y * 2 + h) * NX + x

    ny = nbands // (2 * NX)
    every = [
        (y, h, x, lo, core)
        for y in range(ny)
        for h in range(2)
        for x in range(NX)
        for lo in range(4)
        for core in range(2)
    ]

    def along_z(d):
        pairs = []
        for y, h, x, lo, core in every:
            z = (4 * h + lo + d) % 8
            pairs.append((index(y, h, x, lo, core), index(y, z // 4, x, z % 4, core)))
        return pairs

    return (
        along_z(1),
        along_z(-1),
        [(index(*q), index(q[0], q[1], q[2] ^ 1, q[3], q[4])) for q in every],
        [(index(*q), index(q[0] ^ 1, q[1], q[2], q[3], q[4])) for q in every],
        [(index(*q), index(q[0], q[1], q[2], q[3], q[4] ^ 1)) for q in every],
    )


def local(nbands, coefficients, hamiltonian, neighbours, basis_values):
    both = ("elem", "band")
    up, down, over_x, over_y, over_core = routes(nbands)
    elem = lax.axis_index("elem")
    band = lax.axis_index("band")
    lo, core = elem // 2, elem % 2
    pa = (band % NX + band // (2 * NX)) % 2
    pb = 1 - pa

    def move(value, pairs):
        return lax.ppermute(value, both, pairs)

    own_a = fold(hamiltonian, neighbours, pa[None])
    own_b = fold(hamiltonian, neighbours, pb[None])
    from_below = move(own_a, up)
    from_above = move(own_b, down)

    near = jnp.pad(neighbours.astype(BF), ((0, EDGE - 4), (0, NB - 27)))
    turned = turn(coefficients, near)
    groups = [[2 * z + c for z in range(4)] for c in range(2)]
    y_own = lax.all_to_all(turned, "elem", 0, 0, axis_index_groups=groups)
    y_other = move(y_own, over_core)

    far_a = move(from_below, up)
    far_b = move(from_above, down)
    below_b = move(from_below, over_x)
    above_a = move(from_above, over_y)

    pieces = [own_a, own_b, from_below, from_above, far_a, far_b, below_b, above_a]
    swapped = [move(piece, over_core) for piece in pieces]

    def first(z, c, pair):
        return (((lo + z) % 4) * 2 + c) * 4 + 2 * pair

    order = [(0, pa), (0, pb), (3, pa), (1, pb), (2, pa), (2, pb), (3, pb), (1, pa)]
    base = jnp.stack(
        [first(z, core, pair) for z, pair in order]
        + [first(z, 1 - core, pair) for z, pair in order]
        + [core, elem * 4]
    ).astype(jnp.int32)

    def table(y):
        return y[:, 4 * NB : 4 * NB + 4, :27].astype(jnp.int32)

    ids = jnp.stack([table(y_own), table(y_other)], axis=1)
    ids = jnp.where(core == 0, ids, ids[:, ::-1]).reshape(32, 27)

    filtered, partial = filtering(ids, base, pieces + swapped, y_own, y_other, basis_values)
    parts = partial.reshape(4, nbands, POINTS // nbands).swapaxes(0, 1)
    density = jnp.sum(lax.all_to_all(parts, "band", 0, 0), axis=0) / BANDS
    return filtered, density


def solution(mesh):
    return jax.shard_map(
        functools.partial(local, mesh.shape["band"]),
        mesh=mesh,
        in_specs=(
            P("elem", None, "band"),
            P("elem", None, None, None),
            P("elem", None),
            P("elem", None, None),
        ),
        out_specs=(P("elem", None, "band"), P("elem", "band")),
        check_vma=False,
    )
```

```python
import functools

import jax
import jax.numpy as jnp
from jax import lax
from jax.experimental import pallas as pl
from jax.experimental.pallas import tpu as pltpu
from jax.sharding import PartitionSpec as P

BANDS = 8192
NB = 128
POINTS = 4096
PLANES = 8
KDIM = 12 * NB
WIDE = 4 * NB
NX = 4
EDGE = 16
BF = jnp.bfloat16
F32 = jnp.float32
NT = (((1,), (1,)), ((), ()))


def fold_kernel(pair_ref, near_ref, h0_ref, h1_ref, h2_ref, a_ref, b_ref):
    step = pl.program_id(0)
    e = lax.rem(2 * pair_ref[0] + step, 4)
    rows = lax.broadcasted_iota(jnp.int32, (NB, NB), 0)
    cols = lax.broadcasted_iota(jnp.int32, (NB, NB), 1)
    eye = (rows == cols).astype(F32).astype(BF)
    choices = ((1,), (0, 2))

    def write(out_ref):
        for dx, h_ref in enumerate((h0_ref, h1_ref, h2_ref)):
            ids = [
                near_ref[e, 9 * dx + 3 * b[0] + c[0]] for b in choices for c in choices
            ]
            spot = 0
            for b in choices:
                for c in choices:
                    total = None
                    for i in b:
                        for j in c:
                            part = h_ref[0, 3 * i + j].astype(F32)
                            total = part if total is None else total + part
                    turned = lax.dot_general(
                        eye, total.astype(BF), NT, preferred_element_type=F32
                    )
                    rank = jnp.int32(0)
                    for other in range(4):
                        if other != spot:
                            rank = rank + (ids[other] < ids[spot]).astype(jnp.int32)
                    row = pl.multiple_of((4 * dx + rank) * NB, NB)
                    out_ref[0, pl.ds(row, NB), :] = turned.astype(BF)
                    spot += 1

    @pl.when(step < 2)
    def _():
        write(a_ref)

    @pl.when(step >= 2)
    def _():
        write(b_ref)


def fold(hamiltonian, neighbours, pair):
    shape = jax.ShapeDtypeStruct((2, KDIM, NB), BF)
    return pl.pallas_call(
        fold_kernel,
        out_shape=(shape, shape),
        grid_spec=pltpu.PrefetchScalarGridSpec(
            num_scalar_prefetch=2,
            grid=(4,),
            in_specs=[
                pl.BlockSpec(
                    (1, 9, NB, NB),
                    lambda t, pair, near, dx=dx: (lax.rem(2 * pair[0] + t, 4), dx, 0, 0),
                )
                for dx in range(3)
            ],
            out_specs=(
                pl.BlockSpec((1, KDIM, NB), lambda t, pair, near: (jnp.minimum(t, 1), 0, 0)),
                pl.BlockSpec((1, KDIM, NB), lambda t, pair, near: (jnp.maximum(t - 2, 0), 0, 0)),
            ),
        ),
        compiler_params=pltpu.CompilerParams(vmem_limit_bytes=60 * 2**20),
        cost_estimate=pl.CostEstimate(
            flops=4 * 27 * 2 * NB**3, bytes_accessed=5200000, transcendentals=0
        ),
    )(pair, neighbours, hamiltonian, hamiltonian, hamiltonian)


def turn_kernel(y_ref, near_ref, out_ref):
    for e in range(4):
        block = y_ref[e].astype(F32).T.astype(BF)
        for copy in range(4):
            out_ref[copy, pl.ds(e * NB, NB), :] = block
    for copy in range(4):
        out_ref[copy, pl.ds(4 * NB, EDGE), :] = near_ref[...]


def turn(coefficients, near):
    return pl.pallas_call(
        turn_kernel,
        out_shape=jax.ShapeDtypeStruct((4, 4 * NB + EDGE, NB), BF),
        compiler_params=pltpu.CompilerParams(vmem_limit_bytes=16 * 2**20),
    )(coefficients, near)


def parity(band):
    return (band % NX + band // (2 * NX)) % 2


def piece_bases(lo, core, pa):
    pb = 1 - pa
    order = [(0, pa), (0, pb), (3, pa), (1, pb), (2, pa), (2, pb), (3, pb), (1, pa)]
    return [(((lo + z) % 4) * 2 + core) * 4 + 2 * pair for z, pair in order]


def filter_kernel(near_ref, *refs):
    h_refs = refs[:16]
    y_own, y_other, b_ref, filt_ref, dens_ref = refs[16:21]
    hbuf, ybuf, za, zb, bbuf, pid, slot, h_sems, b_sem = refs[21:]
    elem, band = lax.axis_index("elem"), lax.axis_index("band")
    lo, core = elem // 2, elem % 2
    pa = parity(band)
    bases = piece_bases(lo, core, pa) + piece_bases(lo, 1 - core, pa)

    rep = jnp.int32(0)
    for x in range(PLANES):
        ids = [near_ref[rep, 9 + 3 * b + c] for b in (1, 0) for c in (1, 0)]
        following = near_ref[rep, 18 + 4]
        for a, b in ((0, 1), (2, 3), (0, 2), (1, 3), (1, 2)):
            ids[a], ids[b] = jnp.minimum(ids[a], ids[b]), jnp.maximum(ids[a], ids[b])
        for r in range(4):
            slot[ids[r]] = 4 * x + r
        rep = following

    def place(g):
        s = slot[g]
        return s // 4, pl.multiple_of((s % 4) * NB, NB), s

    def h_copy(ref, k, g):
        x, lane, s = place(g)
        return pltpu.make_async_copy(
            ref.at[k], hbuf.at[x, :, pl.ds(lane, NB)], h_sems.at[s]
        )

    for i, ref in enumerate(h_refs):
        for k in range(2):
            h_copy(ref, k, bases[i] + k).start()

    for source, side in ((y_own, core), (y_other, 1 - core)):
        for z in range(4):
            for e in range(4):
                x, lane, _ = place((2 * z + side) * 4 + e)
                block = source[z, pl.ds(e * NB, NB), :]
                ybuf[0, x, :, pl.ds(lane, NB)] = block
                za[x, :, pl.ds(lane, NB)] = block.astype(F32)

    def around(src, x):
        return jnp.concatenate(
            [ybuf[src, (x + 7) % 8], ybuf[src, x], ybuf[src, (x + 1) % 8]], axis=1
        )

    b_copy = pltpu.make_async_copy(b_ref, bbuf, b_sem)
    for step in range(5):
        if step == 1:
            b_copy.start()
        src, dst = step % 2, 1 - step % 2
        past = zb if step % 2 == 0 else za
        for x in range(PLANES):
            if step == 0:
                for r in range(4):
                    pltpu.make_async_copy(
                        h_refs[0].at[0], hbuf.at[x, :, pl.ds(r * NB, NB)], h_sems.at[4 * x + r]
                    ).wait()
            acc = jnp.dot(around(src, x), hbuf[x], preferred_element_type=F32)
            new = acc if step == 0 else 2.0 * acc - past[x]
            past[x] = new
            ybuf[dst, x] = new.astype(BF)

    b_copy.wait()
    mine = elem * 4
    for e in range(4):
        x, lane, _ = place(mine + e)
        left = lax.rem(x + 7, 8)
        right = lax.rem(x + 1, 8)
        near = jnp.concatenate([ybuf[1, left], ybuf[1, x], ybuf[1, right]], axis=1)
        acc = jnp.dot(near, hbuf[x, :, pl.ds(lane, NB)], preferred_element_type=F32)
        last = (2.0 * acc - za[x, :, pl.ds(lane, NB)]).astype(BF)
        filt_ref[e] = last.astype(F32).T.astype(BF)
        for p in range(0, POINTS, 512):
            phi = lax.dot_general(
                last, bbuf[e, pl.ds(p, 512), :], NT, preferred_element_type=F32
            )
            dens_ref[e : e + 1, p : p + 512] = jnp.sum(phi * phi, axis=0, keepdims=True)


def filtering(near, pieces, y_own, y_other, basis_values):
    anywhere = pl.BlockSpec(memory_space=pl.ANY)
    hbm = pl.BlockSpec(memory_space=pltpu.HBM)
    smem = pl.BlockSpec(memory_space=pltpu.SMEM)
    vmem = pl.BlockSpec(memory_space=pltpu.VMEM)
    return pl.pallas_call(
        filter_kernel,
        out_shape=(
            jax.ShapeDtypeStruct((4, NB, NB), BF),
            jax.ShapeDtypeStruct((4, POINTS), F32),
        ),
        in_specs=[smem, hbm, hbm] + [anywhere] * 14 + [vmem, vmem, anywhere],
        out_specs=(vmem, vmem),
        scratch_shapes=[
            pltpu.VMEM((PLANES, KDIM, WIDE), BF),
            pltpu.VMEM((2, PLANES, NB, WIDE), BF),
            pltpu.VMEM((PLANES, NB, WIDE), F32),
            pltpu.VMEM((PLANES, NB, WIDE), F32),
            pltpu.VMEM((4, POINTS, NB), BF),
            pltpu.SMEM((32,), jnp.int32),
            pltpu.SMEM((32,), jnp.int32),
            pltpu.SemaphoreType.DMA((32,)),
            pltpu.SemaphoreType.DMA,
        ],
        compiler_params=pltpu.CompilerParams(vmem_limit_bytes=40 * 2**20),
    )(near, *pieces, y_own, y_other, basis_values)


def routes(nbands):
    def index(y, h, x, lo, core):
        return (lo * 2 + core) * nbands + (y * 2 + h) * NX + x

    ny = nbands // (2 * NX)
    every = [
        (y, h, x, lo, core)
        for y in range(ny)
        for h in range(2)
        for x in range(NX)
        for lo in range(4)
        for core in range(2)
    ]

    def along_z(d):
        pairs = []
        for y, h, x, lo, core in every:
            z = (4 * h + lo + d) % 8
            pairs.append((index(y, h, x, lo, core), index(y, z // 4, x, z % 4, core)))
        return pairs

    return (
        along_z(1),
        along_z(-1),
        [(index(*q), index(q[0], q[1], q[2] ^ 1, q[3], q[4])) for q in every],
        [(index(*q), index(q[0] ^ 1, q[1], q[2], q[3], q[4])) for q in every],
        [(index(*q), index(q[0], q[1], q[2], q[3], q[4] ^ 1)) for q in every],
    )


def local(nbands, coefficients, hamiltonian, neighbours, basis_values):
    both = ("elem", "band")
    up, down, over_x, over_y, over_core = routes(nbands)
    core = lax.axis_index("elem") % 2
    pa = parity(lax.axis_index("band"))

    def move(value, pairs):
        return lax.ppermute(value, both, pairs)

    own_a, own_b = fold(hamiltonian, neighbours, pa[None])
    from_below = move(own_a, up)
    from_above = move(own_b, down)

    coefficients, neighbours, own_b = lax.optimization_barrier(
        (coefficients, neighbours, own_b)
    )
    near = jnp.pad(neighbours.astype(BF), ((0, EDGE - 4), (0, NB - 27)))
    turned = turn(coefficients, near)
    groups = [[2 * z + c for z in range(4)] for c in range(2)]
    y_own = lax.all_to_all(turned, "elem", 0, 0, axis_index_groups=groups)
    y_other = move(y_own, over_core)

    own_swapped = [move(own_a, over_core), move(own_b, over_core)]
    from_below, from_above, y_other, own_swapped = lax.optimization_barrier(
        (from_below, from_above, y_other, own_swapped)
    )
    far_a = move(from_below, up)
    far_b = move(from_above, down)
    next_swapped = [move(from_below, over_core), move(from_above, over_core)]
    for_x, for_y, next_swapped = lax.optimization_barrier(
        (from_below, from_above, next_swapped)
    )
    below_b = move(for_x, over_x)
    above_a = move(for_y, over_y)


    def table(y):
        return y[:, 4 * NB : 4 * NB + 4, :27].astype(jnp.int32)

    ids = jnp.stack([table(y_own), table(y_other)], axis=1)
    ids = jnp.where(core == 0, ids, ids[:, ::-1]).reshape(32, 27)

    ids, below_b = lax.optimization_barrier((ids, below_b))
    pieces = [own_a, own_b, from_below, from_above, far_a, far_b, below_b, above_a]
    swapped = own_swapped + next_swapped + [move(piece, over_core) for piece in pieces[4:]]

    filtered, partial = filtering(ids, pieces + swapped, y_own, y_other, basis_values)
    parts = partial.reshape(4, nbands, POINTS // nbands).swapaxes(0, 1)
    density = jnp.sum(lax.all_to_all(parts, "band", 0, 0), axis=0) / BANDS
    return filtered, density


def solution(mesh):
    return jax.shard_map(
        functools.partial(local, mesh.shape["band"]),
        mesh=mesh,
        in_specs=(
            P("elem", None, "band"),
            P("elem", None, None, None),
            P("elem", None),
            P("elem", None, None),
        ),
        out_specs=(P("elem", None, "band"), P("elem", "band")),
        check_vma=False,
    )
```

```python
import functools

import jax
import jax.numpy as jnp
from jax import lax
from jax.experimental import pallas as pl
from jax.experimental.pallas import tpu as pltpu
from jax.sharding import PartitionSpec as P

BANDS = 8192
NB = 128
POINTS = 4096
PLANES = 8
KDIM = 12 * NB
WIDE = 4 * NB
NX = 4
EDGE = 16
BF = jnp.bfloat16
F32 = jnp.float32
NT = (((1,), (1,)), ((), ()))


def fold_kernel(pair_ref, near_ref, h_ref, out_ref, hbuf, sems):
    first = 2 * pair_ref[0]
    copies = [
        pltpu.make_async_copy(
            h_ref.at[first + k, pl.ds(9 * dx, 9)], hbuf.at[k, dx], sems.at[k, dx]
        )
        for k in range(2)
        for dx in range(3)
    ]
    for copy in copies:
        copy.start()
    rows = lax.broadcasted_iota(jnp.int32, (NB, NB), 0)
    cols = lax.broadcasted_iota(jnp.int32, (NB, NB), 1)
    eye = (rows == cols).astype(F32).astype(BF)
    choices = ((1,), (0, 2))
    for k in range(2):
        for dx in range(3):
            copies[3 * k + dx].wait()
            ids = [
                near_ref[first + k, 9 * dx + 3 * b[0] + c[0]] for b in choices for c in choices
            ]
            spot = 0
            for b in choices:
                for c in choices:
                    total = None
                    for i in b:
                        for j in c:
                            part = lax.dot_general(
                                eye, hbuf[k, dx, 3 * i + j], NT, preferred_element_type=F32
                            )
                            total = part if total is None else total + part
                    rank = jnp.int32(0)
                    for other in range(4):
                        if other != spot:
                            rank = rank + (ids[other] < ids[spot]).astype(jnp.int32)
                    row = pl.multiple_of((4 * dx + rank) * NB, NB)
                    out_ref[k, pl.ds(row, NB), :] = total.astype(BF)
                    spot += 1


def fold(hamiltonian, neighbours, pair):
    smem = pl.BlockSpec(memory_space=pltpu.SMEM)
    return pl.pallas_call(
        fold_kernel,
        out_shape=jax.ShapeDtypeStruct((2, KDIM, NB), BF),
        in_specs=[smem, smem, pl.BlockSpec(memory_space=pltpu.HBM)],
        out_specs=pl.BlockSpec(memory_space=pltpu.VMEM),
        scratch_shapes=[
            pltpu.VMEM((2, 3, 9, NB, NB), BF),
            pltpu.SemaphoreType.DMA((2, 3)),
        ],
        compiler_params=pltpu.CompilerParams(vmem_limit_bytes=60 * 2**20),
        cost_estimate=pl.CostEstimate(
            flops=2 * 27 * 2 * NB**3, bytes_accessed=2600000, transcendentals=0
        ),
    )(pair, neighbours, hamiltonian)


def turn_kernel(y_ref, near_ref, out_ref):
    for e in range(4):
        block = y_ref[e].astype(F32).T.astype(BF)
        for copy in range(4):
            out_ref[copy, pl.ds(e * NB, NB), :] = block
    for copy in range(4):
        out_ref[copy, pl.ds(4 * NB, EDGE), :] = near_ref[...]


def turn(coefficients, near):
    return pl.pallas_call(
        turn_kernel,
        out_shape=jax.ShapeDtypeStruct((4, 4 * NB + EDGE, NB), BF),
        compiler_params=pltpu.CompilerParams(vmem_limit_bytes=16 * 2**20),
    )(coefficients, near)


def parity(band):
    return (band % NX + band // (2 * NX)) % 2


def piece_bases(lo, core, pa):
    pb = 1 - pa
    order = [(0, pa), (0, pb), (3, pa), (1, pb), (2, pa), (2, pb), (3, pb), (1, pa)]
    return [(((lo + z) % 4) * 2 + core) * 4 + 2 * pair for z, pair in order]


def filter_kernel(near_ref, *refs):
    h_refs = refs[:16]
    y_own, y_other, b_ref, filt_ref, dens_ref = refs[16:21]
    hbuf, ybuf, za, zb, bbuf, pid, slot, h_sems, b_sem = refs[21:]
    elem, band = lax.axis_index("elem"), lax.axis_index("band")
    lo, core = elem // 2, elem % 2
    pa = parity(band)
    bases = piece_bases(lo, core, pa) + piece_bases(lo, 1 - core, pa)

    rep = jnp.int32(0)
    for x in range(PLANES):
        ids = [near_ref[rep, 9 + 3 * b + c] for b in (1, 0) for c in (1, 0)]
        following = near_ref[rep, 18 + 4]
        for a, b in ((0, 1), (2, 3), (0, 2), (1, 3), (1, 2)):
            ids[a], ids[b] = jnp.minimum(ids[a], ids[b]), jnp.maximum(ids[a], ids[b])
        for r in range(4):
            slot[ids[r]] = 4 * x + r
        rep = following

    def place(g):
        s = slot[g]
        return s // 4, pl.multiple_of((s % 4) * NB, NB), s

    def h_copy(ref, k, g):
        x, lane, s = place(g)
        return pltpu.make_async_copy(
            ref.at[k], hbuf.at[x, :, pl.ds(lane, NB)], h_sems.at[s]
        )

    for i, ref in enumerate(h_refs):
        for k in range(2):
            h_copy(ref, k, bases[i] + k).start()

    for source, side in ((y_own, core), (y_other, 1 - core)):
        for z in range(4):
            for e in range(4):
                x, lane, _ = place((2 * z + side) * 4 + e)
                block = source[z, pl.ds(e * NB, NB), :]
                ybuf[0, x, :, pl.ds(lane, NB)] = block
                za[x, :, pl.ds(lane, NB)] = block.astype(F32)

    def around(src, x):
        return jnp.concatenate(
            [ybuf[src, (x + 7) % 8], ybuf[src, x], ybuf[src, (x + 1) % 8]], axis=1
        )

    b_copy = pltpu.make_async_copy(b_ref, bbuf, b_sem)
    for step in range(5):
        if step == 1:
            b_copy.start()
        src, dst = step % 2, 1 - step % 2
        past = zb if step % 2 == 0 else za
        for x in range(PLANES):
            if step == 0:
                for r in range(4):
                    pltpu.make_async_copy(
                        h_refs[0].at[0], hbuf.at[x, :, pl.ds(r * NB, NB)], h_sems.at[4 * x + r]
                    ).wait()
            acc = jnp.dot(around(src, x), hbuf[x], preferred_element_type=F32)
            new = acc if step == 0 else 2.0 * acc - past[x]
            past[x] = new
            ybuf[dst, x] = new.astype(BF)

    b_copy.wait()
    mine = elem * 4
    for e in range(4):
        x, lane, _ = place(mine + e)
        left = lax.rem(x + 7, 8)
        right = lax.rem(x + 1, 8)
        near = jnp.concatenate([ybuf[1, left], ybuf[1, x], ybuf[1, right]], axis=1)
        acc = jnp.dot(near, hbuf[x, :, pl.ds(lane, NB)], preferred_element_type=F32)
        last = (2.0 * acc - za[x, :, pl.ds(lane, NB)]).astype(BF)
        filt_ref[e] = last.astype(F32).T.astype(BF)
        for p in range(0, POINTS, 512):
            phi = lax.dot_general(
                last, bbuf[e, pl.ds(p, 512), :], NT, preferred_element_type=F32
            )
            total = jnp.sum(phi * phi, axis=0, keepdims=True)
            dens_ref[e : e + 1, p : p + 512] = total * (1.0 / BANDS)


def filtering(near, pieces, y_own, y_other, basis_values):
    anywhere = pl.BlockSpec(memory_space=pl.ANY)
    hbm = pl.BlockSpec(memory_space=pltpu.HBM)
    smem = pl.BlockSpec(memory_space=pltpu.SMEM)
    vmem = pl.BlockSpec(memory_space=pltpu.VMEM)
    return pl.pallas_call(
        filter_kernel,
        out_shape=(
            jax.ShapeDtypeStruct((4, NB, NB), BF),
            jax.ShapeDtypeStruct((4, POINTS), F32),
        ),
        in_specs=[smem, hbm, hbm] + [anywhere] * 14 + [vmem, vmem, anywhere],
        out_specs=(vmem, vmem),
        scratch_shapes=[
            pltpu.VMEM((PLANES, KDIM, WIDE), BF),
            pltpu.VMEM((2, PLANES, NB, WIDE), BF),
            pltpu.VMEM((PLANES, NB, WIDE), F32),
            pltpu.VMEM((PLANES, NB, WIDE), F32),
            pltpu.VMEM((4, POINTS, NB), BF),
            pltpu.SMEM((32,), jnp.int32),
            pltpu.SMEM((32,), jnp.int32),
            pltpu.SemaphoreType.DMA((32,)),
            pltpu.SemaphoreType.DMA,
        ],
        compiler_params=pltpu.CompilerParams(vmem_limit_bytes=38 * 2**20),
    )(near, *pieces, y_own, y_other, basis_values)


def total_kernel(parts_ref, out_ref):
    out_ref[...] = jnp.sum(parts_ref[...], axis=0)


def total_of(parts):
    return pl.pallas_call(
        total_kernel, out_shape=jax.ShapeDtypeStruct(parts.shape[1:], F32)
    )(parts)


def routes(nbands):
    def index(y, h, x, lo, core):
        return (lo * 2 + core) * nbands + (y * 2 + h) * NX + x

    ny = nbands // (2 * NX)
    every = [
        (y, h, x, lo, core)
        for y in range(ny)
        for h in range(2)
        for x in range(NX)
        for lo in range(4)
        for core in range(2)
    ]

    def along_z(d):
        pairs = []
        for y, h, x, lo, core in every:
            z = (4 * h + lo + d) % 8
            pairs.append((index(y, h, x, lo, core), index(y, z // 4, x, z % 4, core)))
        return pairs

    return (
        along_z(1),
        along_z(-1),
        [(index(*q), index(q[0], q[1], q[2] ^ 1, q[3], q[4])) for q in every],
        [(index(*q), index(q[0] ^ 1, q[1], q[2], q[3], q[4])) for q in every],
        [(index(*q), index(q[0], q[1], q[2], q[3], q[4] ^ 1)) for q in every],
    )


def local(nbands, coefficients, hamiltonian, neighbours, basis_values):
    both = ("elem", "band")
    up, down, over_x, over_y, over_core = routes(nbands)
    core = lax.axis_index("elem") % 2
    pa = parity(lax.axis_index("band"))

    def move(value, pairs):
        return lax.ppermute(value, both, pairs)

    own_a = fold(hamiltonian, neighbours, pa[None])
    own_b = fold(hamiltonian, neighbours, 1 - pa[None])
    from_below = move(own_a, up)
    from_above = move(own_b, down)

    coefficients, neighbours, own_b = lax.optimization_barrier(
        (coefficients, neighbours, own_b)
    )
    near = jnp.pad(neighbours.astype(BF), ((0, EDGE - 4), (0, NB - 27)))
    turned = turn(coefficients, near)
    groups = [[2 * z + c for z in range(4)] for c in range(2)]
    y_own = lax.all_to_all(turned, "elem", 0, 0, axis_index_groups=groups)
    y_other = move(y_own, over_core)

    own_a, own_b, y_own = lax.optimization_barrier((own_a, own_b, y_own))
    own_swapped = [move(own_a, over_core), move(own_b, over_core)]
    from_below, from_above, y_other, own_swapped = lax.optimization_barrier(
        (from_below, from_above, y_other, own_swapped)
    )
    far_a = move(from_below, up)
    far_b = move(from_above, down)
    below_b = move(from_below, over_x)
    above_a = move(from_above, over_y)


    def table(y):
        return y[:, 4 * NB : 4 * NB + 4, :27].astype(jnp.int32)

    ids = jnp.stack([table(y_own), table(y_other)], axis=1)
    ids = jnp.where(core == 0, ids, ids[:, ::-1]).reshape(32, 27)

    ids, below_b = lax.optimization_barrier((ids, below_b))
    pieces = [own_a, own_b, from_below, from_above, far_a, far_b, below_b, above_a]
    swapped = own_swapped + [move(piece, over_core) for piece in pieces[2:]]

    filtered, partial = filtering(ids, pieces + swapped, y_own, y_other, basis_values)
    parts = partial.reshape(4, nbands, POINTS // nbands).swapaxes(0, 1)
    density = total_of(lax.all_to_all(parts, "band", 0, 0))
    return filtered, density


def solution(mesh):
    return jax.shard_map(
        functools.partial(local, mesh.shape["band"]),
        mesh=mesh,
        in_specs=(
            P("elem", None, "band"),
            P("elem", None, None, None),
            P("elem", None),
            P("elem", None, None),
        ),
        out_specs=(P("elem", None, "band"), P("elem", "band")),
        check_vma=False,
    )
```

```python
import functools

import jax
import jax.numpy as jnp
from jax import lax
from jax.experimental import pallas as pl
from jax.experimental.pallas import tpu as pltpu
from jax.sharding import PartitionSpec as P

BANDS = 8192
NB = 128
POINTS = 4096
PLANES = 8
KDIM = 12 * NB
WIDE = 4 * NB
NX = 4
EDGE = 16
BF = jnp.bfloat16
F32 = jnp.float32
NT = (((1,), (1,)), ((), ()))


def fold_kernel(pair_ref, near_ref, h0_ref, h1_ref, h2_ref, a_ref, b_ref):
    step = pl.program_id(0)
    e = lax.rem(2 * pair_ref[0] + step, 4)
    rows = lax.broadcasted_iota(jnp.int32, (NB, NB), 0)
    cols = lax.broadcasted_iota(jnp.int32, (NB, NB), 1)
    eye = (rows == cols).astype(F32).astype(BF)
    choices = ((1,), (0, 2))

    def write(out_ref):
        for dx, h_ref in enumerate((h0_ref, h1_ref, h2_ref)):
            ids = [
                near_ref[e, 9 * dx + 3 * b[0] + c[0]] for b in choices for c in choices
            ]
            spot = 0
            for b in choices:
                for c in choices:
                    total = None
                    for i in b:
                        for j in c:
                            part = h_ref[0, 3 * i + j].astype(F32)
                            total = part if total is None else total + part
                    turned = lax.dot_general(
                        eye, total.astype(BF), NT, preferred_element_type=F32
                    )
                    rank = jnp.int32(0)
                    for other in range(4):
                        if other != spot:
                            rank = rank + (ids[other] < ids[spot]).astype(jnp.int32)
                    row = pl.multiple_of((4 * dx + rank) * NB, NB)
                    out_ref[0, pl.ds(row, NB), :] = turned.astype(BF)
                    spot += 1

    @pl.when(step < 2)
    def _():
        write(a_ref)

    @pl.when(step >= 2)
    def _():
        write(b_ref)


def fold(hamiltonian, neighbours, pair):
    shape = jax.ShapeDtypeStruct((2, KDIM, NB), BF)
    return pl.pallas_call(
        fold_kernel,
        out_shape=(shape, shape),
        grid_spec=pltpu.PrefetchScalarGridSpec(
            num_scalar_prefetch=2,
            grid=(4,),
            in_specs=[
                pl.BlockSpec(
                    (1, 9, NB, NB),
                    lambda t, pair, near, dx=dx: (lax.rem(2 * pair[0] + t, 4), dx, 0, 0),
                )
                for dx in range(3)
            ],
            out_specs=(
                pl.BlockSpec((1, KDIM, NB), lambda t, pair, near: (jnp.minimum(t, 1), 0, 0)),
                pl.BlockSpec((1, KDIM, NB), lambda t, pair, near: (jnp.maximum(t - 2, 0), 0, 0)),
            ),
        ),
        compiler_params=pltpu.CompilerParams(vmem_limit_bytes=16 * 2**20),
        cost_estimate=pl.CostEstimate(
            flops=4 * 27 * 2 * NB**3, bytes_accessed=5200000, transcendentals=0
        ),
    )(pair, neighbours, hamiltonian, hamiltonian, hamiltonian)


def turn_kernel(y_ref, near_ref, out_ref):
    for e in range(4):
        block = y_ref[e].astype(F32).T.astype(BF)
        for copy in range(4):
            out_ref[copy, pl.ds(e * NB, NB), :] = block
    for copy in range(4):
        out_ref[copy, pl.ds(4 * NB, EDGE), :] = near_ref[...]


def turn(coefficients, near):
    return pl.pallas_call(
        turn_kernel,
        out_shape=jax.ShapeDtypeStruct((4, 4 * NB + EDGE, NB), BF),
        compiler_params=pltpu.CompilerParams(vmem_limit_bytes=16 * 2**20),
    )(coefficients, near)


def parity(band):
    return (band % NX + band // (2 * NX)) % 2


def piece_bases(lo, core, pa):
    pb = 1 - pa
    order = [(0, pa), (0, pb), (3, pa), (1, pb), (2, pa), (2, pb), (3, pb), (1, pa)]
    return [(((lo + z) % 4) * 2 + core) * 4 + 2 * pair for z, pair in order]


def filter_kernel(near_ref, *refs):
    h_refs = refs[:16]
    y_own, y_other, b_ref, filt_ref, dens_ref = refs[16:21]
    hbuf, ybuf, za, zb, bbuf, pid, slot, h_sems, b_sem = refs[21:]
    elem, band = lax.axis_index("elem"), lax.axis_index("band")
    lo, core = elem // 2, elem % 2
    pa = parity(band)
    bases = piece_bases(lo, core, pa) + piece_bases(lo, 1 - core, pa)

    rep = jnp.int32(0)
    for x in range(PLANES):
        ids = [near_ref[rep, 9 + 3 * b + c] for b in (1, 0) for c in (1, 0)]
        following = near_ref[rep, 18 + 4]
        for a, b in ((0, 1), (2, 3), (0, 2), (1, 3), (1, 2)):
            ids[a], ids[b] = jnp.minimum(ids[a], ids[b]), jnp.maximum(ids[a], ids[b])
        for r in range(4):
            slot[ids[r]] = 4 * x + r
        rep = following

    def place(g):
        s = slot[g]
        return s // 4, pl.multiple_of((s % 4) * NB, NB), s

    def h_copy(ref, k, g):
        x, lane, s = place(g)
        return pltpu.make_async_copy(
            ref.at[k], hbuf.at[x, :, pl.ds(lane, NB)], h_sems.at[s]
        )

    for i, ref in enumerate(h_refs):
        for k in range(2):
            h_copy(ref, k, bases[i] + k).start()

    for source, side in ((y_own, core), (y_other, 1 - core)):
        for z in range(4):
            for e in range(4):
                x, lane, _ = place((2 * z + side) * 4 + e)
                block = source[z, pl.ds(e * NB, NB), :]
                ybuf[0, x, :, pl.ds(lane, NB)] = block
                za[x, :, pl.ds(lane, NB)] = block.astype(F32)

    def around(src, x):
        return jnp.concatenate(
            [ybuf[src, (x + 7) % 8], ybuf[src, x], ybuf[src, (x + 1) % 8]], axis=1
        )

    b_copy = pltpu.make_async_copy(b_ref, bbuf, b_sem)
    for step in range(5):
        if step == 1:
            b_copy.start()
        src, dst = step % 2, 1 - step % 2
        past = zb if step % 2 == 0 else za
        for x in range(PLANES):
            if step == 0:
                for r in range(4):
                    pltpu.make_async_copy(
                        h_refs[0].at[0], hbuf.at[x, :, pl.ds(r * NB, NB)], h_sems.at[4 * x + r]
                    ).wait()
            acc = jnp.dot(around(src, x), hbuf[x], preferred_element_type=F32)
            new = acc if step == 0 else 2.0 * acc - past[x]
            past[x] = new
            ybuf[dst, x] = new.astype(BF)

    b_copy.wait()
    mine = elem * 4
    for e in range(4):
        x, lane, _ = place(mine + e)
        left = lax.rem(x + 7, 8)
        right = lax.rem(x + 1, 8)
        near = jnp.concatenate([ybuf[1, left], ybuf[1, x], ybuf[1, right]], axis=1)
        acc = jnp.dot(near, hbuf[x, :, pl.ds(lane, NB)], preferred_element_type=F32)
        last = (2.0 * acc - za[x, :, pl.ds(lane, NB)]).astype(BF)
        filt_ref[e] = last.astype(F32).T.astype(BF)
        for p in range(0, POINTS, 512):
            phi = lax.dot_general(
                last, bbuf[e, pl.ds(p, 512), :], NT, preferred_element_type=F32
            )
            total = jnp.sum(phi * phi, axis=0, keepdims=True)
            dens_ref[e : e + 1, p : p + 512] = total * (1.0 / BANDS)


def filtering(near, pieces, y_own, y_other, basis_values):
    anywhere = pl.BlockSpec(memory_space=pl.ANY)
    hbm = pl.BlockSpec(memory_space=pltpu.HBM)
    smem = pl.BlockSpec(memory_space=pltpu.SMEM)
    vmem = pl.BlockSpec(memory_space=pltpu.VMEM)
    return pl.pallas_call(
        filter_kernel,
        out_shape=(
            jax.ShapeDtypeStruct((4, NB, NB), BF),
            jax.ShapeDtypeStruct((4, POINTS), F32),
        ),
        in_specs=[smem, hbm, hbm] + [anywhere] * 14 + [vmem, vmem, anywhere],
        out_specs=(vmem, vmem),
        scratch_shapes=[
            pltpu.VMEM((PLANES, KDIM, WIDE), BF),
            pltpu.VMEM((2, PLANES, NB, WIDE), BF),
            pltpu.VMEM((PLANES, NB, WIDE), F32),
            pltpu.VMEM((PLANES, NB, WIDE), F32),
            pltpu.VMEM((4, POINTS, NB), BF),
            pltpu.SMEM((32,), jnp.int32),
            pltpu.SMEM((32,), jnp.int32),
            pltpu.SemaphoreType.DMA((32,)),
            pltpu.SemaphoreType.DMA,
        ],
        compiler_params=pltpu.CompilerParams(vmem_limit_bytes=38 * 2**20),
    )(near, *pieces, y_own, y_other, basis_values)


def routes(nbands):
    def index(y, h, x, lo, core):
        return (lo * 2 + core) * nbands + (y * 2 + h) * NX + x

    ny = nbands // (2 * NX)
    every = [
        (y, h, x, lo, core)
        for y in range(ny)
        for h in range(2)
        for x in range(NX)
        for lo in range(4)
        for core in range(2)
    ]

    def along_z(d):
        pairs = []
        for y, h, x, lo, core in every:
            z = (4 * h + lo + d) % 8
            pairs.append((index(y, h, x, lo, core), index(y, z // 4, x, z % 4, core)))
        return pairs

    return (
        along_z(1),
        along_z(-1),
        [(index(*q), index(q[0], q[1], q[2] ^ 1, q[3], q[4])) for q in every],
        [(index(*q), index(q[0] ^ 1, q[1], q[2], q[3], q[4])) for q in every],
        [(index(*q), index(q[0], q[1], q[2], q[3], q[4] ^ 1)) for q in every],
    )


def local(nbands, coefficients, hamiltonian, neighbours, basis_values):
    both = ("elem", "band")
    up, down, over_x, over_y, over_core = routes(nbands)
    core = lax.axis_index("elem") % 2
    pa = parity(lax.axis_index("band"))

    def move(value, pairs):
        return lax.ppermute(value, both, pairs)

    own_a, own_b = fold(hamiltonian, neighbours, pa[None])
    from_below = move(own_a, up)
    from_above = move(own_b, down)

    near = jnp.pad(neighbours.astype(BF), ((0, EDGE - 4), (0, NB - 27)))
    turned = turn(coefficients, near)
    groups = [[2 * z + c for z in range(4)] for c in range(2)]
    y_own = lax.all_to_all(turned, "elem", 0, 0, axis_index_groups=groups)
    y_other = move(y_own, over_core)

    own_swapped = [move(own_a, over_core), move(own_b, over_core)]
    from_above, y_other, own_swapped = lax.optimization_barrier(
        (from_above, y_other, own_swapped)
    )
    far_a = move(from_below, up)
    far_b = move(from_above, down)
    below_b = move(from_below, over_x)
    above_a = move(from_above, over_y)


    def table(y):
        return y[:, 4 * NB : 4 * NB + 4, :27].astype(jnp.int32)

    ids = jnp.stack([table(y_own), table(y_other)], axis=1)
    ids = jnp.where(core == 0, ids, ids[:, ::-1]).reshape(32, 27)

    ids, below_b = lax.optimization_barrier((ids, below_b))
    pieces = [own_a, own_b, from_below, from_above, far_a, far_b, below_b, above_a]
    swapped = own_swapped + [move(piece, over_core) for piece in pieces[2:]]

    filtered, partial = filtering(ids, pieces + swapped, y_own, y_other, basis_values)
    points = POINTS // nbands
    parts = partial.reshape(4, nbands, points).swapaxes(0, 1)
    parts = lax.all_to_all(parts.reshape(nbands, points // 32, 128), "band", 0, 0)
    return filtered, jnp.sum(parts, axis=0).reshape(4, points)


def solution(mesh):
    return jax.shard_map(
        functools.partial(local, mesh.shape["band"]),
        mesh=mesh,
        in_specs=(
            P("elem", None, "band"),
            P("elem", None, None, None),
            P("elem", None),
            P("elem", None, None),
        ),
        out_specs=(P("elem", None, "band"), P("elem", "band")),
        check_vma=False,
    )
```

```python
import functools

import jax
import jax.numpy as jnp
from jax import lax
from jax.experimental import pallas as pl
from jax.experimental.pallas import tpu as pltpu
from jax.sharding import PartitionSpec as P

BANDS = 8192
NB = 128
POINTS = 4096
PLANES = 8
KDIM = 12 * NB
WIDE = 4 * NB
NX = 4
EDGE = 16
BF = jnp.bfloat16
F32 = jnp.float32
NT = (((1,), (1,)), ((), ()))


def fold_kernel(pair_ref, near_ref, h0_ref, h1_ref, h2_ref, a_ref, b_ref):
    step = pl.program_id(0)
    e = lax.rem(2 * pair_ref[0] + step, 4)
    rows = lax.broadcasted_iota(jnp.int32, (NB, NB), 0)
    cols = lax.broadcasted_iota(jnp.int32, (NB, NB), 1)
    eye = (rows == cols).astype(F32).astype(BF)
    choices = ((1,), (0, 2))

    def write(out_ref):
        for dx, h_ref in enumerate((h0_ref, h1_ref, h2_ref)):
            ids = [
                near_ref[e, 9 * dx + 3 * b[0] + c[0]] for b in choices for c in choices
            ]
            spot = 0
            for b in choices:
                for c in choices:
                    total = None
                    for i in b:
                        for j in c:
                            part = h_ref[0, 3 * i + j].astype(F32)
                            total = part if total is None else total + part
                    turned = lax.dot_general(
                        eye, total.astype(BF), NT, preferred_element_type=F32
                    )
                    rank = jnp.int32(0)
                    for other in range(4):
                        if other != spot:
                            rank = rank + (ids[other] < ids[spot]).astype(jnp.int32)
                    row = pl.multiple_of((4 * dx + rank) * NB, NB)
                    out_ref[0, pl.ds(row, NB), :] = turned.astype(BF)
                    spot += 1

    @pl.when(step < 2)
    def _():
        write(a_ref)

    @pl.when(step >= 2)
    def _():
        write(b_ref)


def fold(hamiltonian, neighbours, pair):
    shape = jax.ShapeDtypeStruct((2, KDIM, NB), BF)
    return pl.pallas_call(
        fold_kernel,
        out_shape=(shape, shape),
        grid_spec=pltpu.PrefetchScalarGridSpec(
            num_scalar_prefetch=2,
            grid=(4,),
            in_specs=[
                pl.BlockSpec(
                    (1, 9, NB, NB),
                    lambda t, pair, near, dx=dx: (lax.rem(2 * pair[0] + t, 4), dx, 0, 0),
                )
                for dx in range(3)
            ],
            out_specs=(
                pl.BlockSpec((1, KDIM, NB), lambda t, pair, near: (jnp.minimum(t, 1), 0, 0)),
                pl.BlockSpec((1, KDIM, NB), lambda t, pair, near: (jnp.maximum(t - 2, 0), 0, 0)),
            ),
        ),
        compiler_params=pltpu.CompilerParams(vmem_limit_bytes=16 * 2**20),
        cost_estimate=pl.CostEstimate(
            flops=4 * 27 * 2 * NB**3, bytes_accessed=5200000, transcendentals=0
        ),
    )(pair, neighbours, hamiltonian, hamiltonian, hamiltonian)


def turn_kernel(y_ref, near_ref, out_ref):
    for e in range(4):
        block = y_ref[e].astype(F32).T.astype(BF)
        for copy in range(4):
            out_ref[copy, pl.ds(e * NB, NB), :] = block
    for copy in range(4):
        out_ref[copy, pl.ds(4 * NB, EDGE), :] = near_ref[...]


def turn(coefficients, near):
    return pl.pallas_call(
        turn_kernel,
        out_shape=jax.ShapeDtypeStruct((4, 4 * NB + EDGE, NB), BF),
        compiler_params=pltpu.CompilerParams(vmem_limit_bytes=16 * 2**20),
    )(coefficients, near)


def parity(band):
    return (band % NX + band // (2 * NX)) % 2


def piece_bases(lo, core, pa):
    pb = 1 - pa
    order = [(0, pa), (0, pb), (3, pa), (1, pb), (2, pa), (2, pb), (3, pb), (1, pa)]
    return [(((lo + z) % 4) * 2 + core) * 4 + 2 * pair for z, pair in order]


def filter_kernel(near_ref, *refs):
    h_refs = refs[:16]
    y_own, y_other, b_ref, filt_ref, dens_ref = refs[16:21]
    hbuf, ybuf, za, zb, bbuf, pid, slot, h_sems, b_sem = refs[21:]
    elem, band = lax.axis_index("elem"), lax.axis_index("band")
    lo, core = elem // 2, elem % 2
    pa = parity(band)
    bases = piece_bases(lo, core, pa) + piece_bases(lo, 1 - core, pa)

    rep = jnp.int32(0)
    for x in range(PLANES):
        ids = [near_ref[rep, 9 + 3 * b + c] for b in (1, 0) for c in (1, 0)]
        following = near_ref[rep, 18 + 4]
        for a, b in ((0, 1), (2, 3), (0, 2), (1, 3), (1, 2)):
            ids[a], ids[b] = jnp.minimum(ids[a], ids[b]), jnp.maximum(ids[a], ids[b])
        for r in range(4):
            slot[ids[r]] = 4 * x + r
        rep = following

    def place(g):
        s = slot[g]
        return s // 4, pl.multiple_of((s % 4) * NB, NB), s

    def h_copy(ref, k, g):
        x, lane, s = place(g)
        return pltpu.make_async_copy(
            ref.at[k], hbuf.at[x, :, pl.ds(lane, NB)], h_sems.at[s]
        )

    for i, ref in enumerate(h_refs):
        for k in range(2):
            h_copy(ref, k, bases[i] + k).start()

    for source, side in ((y_own, core), (y_other, 1 - core)):
        for z in range(4):
            for e in range(4):
                x, lane, _ = place((2 * z + side) * 4 + e)
                block = source[z, pl.ds(e * NB, NB), :]
                ybuf[0, x, :, pl.ds(lane, NB)] = block
                za[x, :, pl.ds(lane, NB)] = block.astype(F32)

    def around(src, x):
        return jnp.concatenate(
            [ybuf[src, (x + 7) % 8], ybuf[src, x], ybuf[src, (x + 1) % 8]], axis=1
        )

    b_copy = pltpu.make_async_copy(b_ref, bbuf, b_sem)
    for step in range(5):
        if step == 1:
            b_copy.start()
        src, dst = step % 2, 1 - step % 2
        past = zb if step % 2 == 0 else za
        for x in range(PLANES):
            if step == 0:
                for r in range(4):
                    pltpu.make_async_copy(
                        h_refs[0].at[0], hbuf.at[x, :, pl.ds(r * NB, NB)], h_sems.at[4 * x + r]
                    ).wait()
            acc = jnp.dot(around(src, x), hbuf[x], preferred_element_type=F32)
            new = acc if step == 0 else 2.0 * acc - past[x]
            past[x] = new
            ybuf[dst, x] = new.astype(BF)

    b_copy.wait()
    mine = elem * 4
    for e in range(4):
        x, lane, _ = place(mine + e)
        left = lax.rem(x + 7, 8)
        right = lax.rem(x + 1, 8)
        near = jnp.concatenate([ybuf[1, left], ybuf[1, x], ybuf[1, right]], axis=1)
        acc = jnp.dot(near, hbuf[x, :, pl.ds(lane, NB)], preferred_element_type=F32)
        last = (2.0 * acc - za[x, :, pl.ds(lane, NB)]).astype(BF)
        filt_ref[e] = last.astype(F32).T.astype(BF)
        for p in range(0, POINTS, 512):
            phi = lax.dot_general(
                last, bbuf[e, pl.ds(p, 512), :], NT, preferred_element_type=F32
            )
            total = jnp.sum(phi * phi, axis=0, keepdims=True)
            dens_ref[e : e + 1, p : p + 512] = total * (1.0 / BANDS)


def filtering(near, pieces, y_own, y_other, basis_values):
    anywhere = pl.BlockSpec(memory_space=pl.ANY)
    hbm = pl.BlockSpec(memory_space=pltpu.HBM)
    smem = pl.BlockSpec(memory_space=pltpu.SMEM)
    vmem = pl.BlockSpec(memory_space=pltpu.VMEM)
    return pl.pallas_call(
        filter_kernel,
        out_shape=(
            jax.ShapeDtypeStruct((4, NB, NB), BF),
            jax.ShapeDtypeStruct((4, POINTS), F32),
        ),
        in_specs=[smem, hbm, hbm] + [anywhere] * 14 + [vmem, vmem, anywhere],
        out_specs=(vmem, vmem),
        scratch_shapes=[
            pltpu.VMEM((PLANES, KDIM, WIDE), BF),
            pltpu.VMEM((2, PLANES, NB, WIDE), BF),
            pltpu.VMEM((PLANES, NB, WIDE), F32),
            pltpu.VMEM((PLANES, NB, WIDE), F32),
            pltpu.VMEM((4, POINTS, NB), BF),
            pltpu.SMEM((32,), jnp.int32),
            pltpu.SMEM((32,), jnp.int32),
            pltpu.SemaphoreType.DMA((32,)),
            pltpu.SemaphoreType.DMA,
        ],
        compiler_params=pltpu.CompilerParams(vmem_limit_bytes=38 * 2**20),
    )(near, *pieces, y_own, y_other, basis_values)


def routes(nbands):
    def index(y, h, x, lo, core):
        return (lo * 2 + core) * nbands + (y * 2 + h) * NX + x

    ny = nbands // (2 * NX)
    every = [
        (y, h, x, lo, core)
        for y in range(ny)
        for h in range(2)
        for x in range(NX)
        for lo in range(4)
        for core in range(2)
    ]

    def along_z(d):
        pairs = []
        for y, h, x, lo, core in every:
            z = (4 * h + lo + d) % 8
            pairs.append((index(y, h, x, lo, core), index(y, z // 4, x, z % 4, core)))
        return pairs

    return (
        along_z(1),
        along_z(-1),
        [(index(*q), index(q[0], q[1], q[2] ^ 1, q[3], q[4])) for q in every],
        [(index(*q), index(q[0] ^ 1, q[1], q[2], q[3], q[4])) for q in every],
        [(index(*q), index(q[0], q[1], q[2], q[3], q[4] ^ 1)) for q in every],
    )


def local(nbands, coefficients, hamiltonian, neighbours, basis_values):
    both = ("elem", "band")
    up, down, over_x, over_y, over_core = routes(nbands)
    core = lax.axis_index("elem") % 2
    pa = parity(lax.axis_index("band"))

    def move(value, pairs):
        return lax.ppermute(value, both, pairs)

    own_a, own_b = fold(hamiltonian, neighbours, pa[None])
    from_below = move(own_a, up)
    from_above = move(own_b, down)

    coefficients, neighbours, own_b = lax.optimization_barrier(
        (coefficients, neighbours, own_b)
    )
    near = jnp.pad(neighbours.astype(BF), ((0, EDGE - 4), (0, NB - 27)))
    turned = turn(coefficients, near)
    groups = [[2 * z + c for z in range(4)] for c in range(2)]
    y_own = lax.all_to_all(turned, "elem", 0, 0, axis_index_groups=groups)
    y_other = move(y_own, over_core)

    own_swapped = [move(own_a, over_core), move(own_b, over_core)]
    from_above, own_swapped = lax.optimization_barrier((from_above, own_swapped))
    far_a = move(from_below, up)
    far_b = move(from_above, down)
    below_b = move(from_below, over_x)
    below_swapped = move(from_below, over_core)
    for_y, below_swapped = lax.optimization_barrier((from_above, below_swapped))
    above_a = move(for_y, over_y)


    def table(y):
        return y[:, 4 * NB : 4 * NB + 4, :27].astype(jnp.int32)

    ids = jnp.stack([table(y_own), table(y_other)], axis=1)
    ids = jnp.where(core == 0, ids, ids[:, ::-1]).reshape(32, 27)

    ids, below_b = lax.optimization_barrier((ids, below_b))
    pieces = [own_a, own_b, from_below, from_above, far_a, far_b, below_b, above_a]
    swapped = own_swapped + [below_swapped] + [move(piece, over_core) for piece in pieces[3:]]

    filtered, partial = filtering(ids, pieces + swapped, y_own, y_other, basis_values)
    points = POINTS // nbands
    parts = partial.reshape(4, nbands, points).swapaxes(0, 1)
    parts = lax.all_to_all(parts.reshape(nbands, points // 32, 128), "band", 0, 0)
    return filtered, jnp.sum(parts, axis=0).reshape(4, points)


def solution(mesh):
    return jax.shard_map(
        functools.partial(local, mesh.shape["band"]),
        mesh=mesh,
        in_specs=(
            P("elem", None, "band"),
            P("elem", None, None, None),
            P("elem", None),
            P("elem", None, None),
        ),
        out_specs=(P("elem", None, "band"), P("elem", "band")),
        check_vma=False,
    )
```

```python
import functools

import jax
import jax.numpy as jnp
from jax import lax
from jax.experimental import pallas as pl
from jax.experimental.pallas import tpu as pltpu
from jax.sharding import PartitionSpec as P

BANDS = 8192
NB = 128
POINTS = 4096
PLANES = 8
KDIM = 12 * NB
WIDE = 4 * NB
NX = 4
EDGE = 16
BF = jnp.bfloat16
F32 = jnp.float32
NT = (((1,), (1,)), ((), ()))


def fold_kernel(pair_ref, near_ref, h0_ref, h1_ref, h2_ref, a_ref, b_ref):
    step = pl.program_id(0)
    e = lax.rem(2 * pair_ref[0] + step, 4)
    rows = lax.broadcasted_iota(jnp.int32, (NB, NB), 0)
    cols = lax.broadcasted_iota(jnp.int32, (NB, NB), 1)
    eye = (rows == cols).astype(F32).astype(BF)
    choices = ((1,), (0, 2))

    def write(out_ref):
        for dx, h_ref in enumerate((h0_ref, h1_ref, h2_ref)):
            ids = [
                near_ref[e, 9 * dx + 3 * b[0] + c[0]] for b in choices for c in choices
            ]
            spot = 0
            for b in choices:
                for c in choices:
                    total = None
                    for i in b:
                        for j in c:
                            part = h_ref[0, 3 * i + j].astype(F32)
                            total = part if total is None else total + part
                    turned = lax.dot_general(
                        eye, total.astype(BF), NT, preferred_element_type=F32
                    )
                    rank = jnp.int32(0)
                    for other in range(4):
                        if other != spot:
                            rank = rank + (ids[other] < ids[spot]).astype(jnp.int32)
                    row = pl.multiple_of((4 * dx + rank) * NB, NB)
                    out_ref[0, pl.ds(row, NB), :] = turned.astype(BF)
                    spot += 1

    @pl.when(step < 2)
    def _():
        write(a_ref)

    @pl.when(step >= 2)
    def _():
        write(b_ref)


def fold(hamiltonian, neighbours, pair):
    shape = jax.ShapeDtypeStruct((2, KDIM, NB), BF)
    return pl.pallas_call(
        fold_kernel,
        out_shape=(shape, shape),
        grid_spec=pltpu.PrefetchScalarGridSpec(
            num_scalar_prefetch=2,
            grid=(4,),
            in_specs=[
                pl.BlockSpec(
                    (1, 9, NB, NB),
                    lambda t, pair, near, dx=dx: (lax.rem(2 * pair[0] + t, 4), dx, 0, 0),
                )
                for dx in range(3)
            ],
            out_specs=(
                pl.BlockSpec((1, KDIM, NB), lambda t, pair, near: (jnp.minimum(t, 1), 0, 0)),
                pl.BlockSpec((1, KDIM, NB), lambda t, pair, near: (jnp.maximum(t - 2, 0), 0, 0)),
            ),
        ),
        compiler_params=pltpu.CompilerParams(vmem_limit_bytes=16 * 2**20),
        cost_estimate=pl.CostEstimate(
            flops=4 * 27 * 2 * NB**3, bytes_accessed=5200000, transcendentals=0
        ),
    )(pair, neighbours, hamiltonian, hamiltonian, hamiltonian)


def turn_kernel(y_ref, near_ref, out_ref):
    for e in range(4):
        block = y_ref[e].astype(F32).T.astype(BF)
        for copy in range(4):
            out_ref[copy, pl.ds(e * NB, NB), :] = block
    for copy in range(4):
        out_ref[copy, pl.ds(4 * NB, EDGE), :] = near_ref[...]


def turn(coefficients, near):
    return pl.pallas_call(
        turn_kernel,
        out_shape=jax.ShapeDtypeStruct((4, 4 * NB + EDGE, NB), BF),
        compiler_params=pltpu.CompilerParams(vmem_limit_bytes=16 * 2**20),
    )(coefficients, near)


def parity(band):
    return (band % NX + band // (2 * NX)) % 2


def piece_bases(lo, core, pa):
    pb = 1 - pa
    order = [(0, pa), (0, pb), (3, pa), (1, pb), (2, pa), (2, pb), (3, pb), (1, pa)]
    return [(((lo + z) % 4) * 2 + core) * 4 + 2 * pair for z, pair in order]


def filter_kernel(near_ref, *refs):
    h_refs = refs[:16]
    y_own, y_other, b_ref, filt_ref, dens_ref = refs[16:21]
    hbuf, ybuf, za, zb, bbuf, pid, slot, h_sems, b_sem = refs[21:]
    elem, band = lax.axis_index("elem"), lax.axis_index("band")
    lo, core = elem // 2, elem % 2
    pa = parity(band)
    bases = piece_bases(lo, core, pa) + piece_bases(lo, 1 - core, pa)

    rep = jnp.int32(0)
    for x in range(PLANES):
        ids = [near_ref[rep, 9 + 3 * b + c] for b in (1, 0) for c in (1, 0)]
        following = near_ref[rep, 18 + 4]
        for a, b in ((0, 1), (2, 3), (0, 2), (1, 3), (1, 2)):
            ids[a], ids[b] = jnp.minimum(ids[a], ids[b]), jnp.maximum(ids[a], ids[b])
        for r in range(4):
            slot[ids[r]] = 4 * x + r
        rep = following

    def place(g):
        s = slot[g]
        return s // 4, pl.multiple_of((s % 4) * NB, NB), s

    def h_copy(ref, k, g):
        x, lane, s = place(g)
        return pltpu.make_async_copy(
            ref.at[k], hbuf.at[x, :, pl.ds(lane, NB)], h_sems.at[s]
        )

    for i, ref in enumerate(h_refs):
        for k in range(2):
            h_copy(ref, k, bases[i] + k).start()

    for source, side in ((y_own, core), (y_other, 1 - core)):
        for z in range(4):
            for e in range(4):
                x, lane, _ = place((2 * z + side) * 4 + e)
                block = source[z, pl.ds(e * NB, NB), :]
                ybuf[0, x, :, pl.ds(lane, NB)] = block
                za[x, :, pl.ds(lane, NB)] = block.astype(F32)

    def around(src, x):
        return jnp.concatenate(
            [ybuf[src, (x + 7) % 8], ybuf[src, x], ybuf[src, (x + 1) % 8]], axis=1
        )

    b_copy = pltpu.make_async_copy(b_ref, bbuf, b_sem)
    for step in range(5):
        if step == 1:
            b_copy.start()
        src, dst = step % 2, 1 - step % 2
        past = zb if step % 2 == 0 else za
        for x in range(PLANES):
            if step == 0:
                for r in range(4):
                    pltpu.make_async_copy(
                        h_refs[0].at[0], hbuf.at[x, :, pl.ds(r * NB, NB)], h_sems.at[4 * x + r]
                    ).wait()
            acc = jnp.dot(around(src, x), hbuf[x], preferred_element_type=F32)
            new = acc if step == 0 else 2.0 * acc - past[x]
            past[x] = new
            ybuf[dst, x] = new.astype(BF)

    b_copy.wait()
    mine = elem * 4
    for e in range(4):
        x, lane, _ = place(mine + e)
        left = lax.rem(x + 7, 8)
        right = lax.rem(x + 1, 8)
        near = jnp.concatenate([ybuf[1, left], ybuf[1, x], ybuf[1, right]], axis=1)
        acc = jnp.dot(near, hbuf[x, :, pl.ds(lane, NB)], preferred_element_type=F32)
        last = (2.0 * acc - za[x, :, pl.ds(lane, NB)]).astype(BF)
        filt_ref[e] = last.astype(F32).T.astype(BF)
        for p in range(0, POINTS, 512):
            phi = lax.dot_general(
                last, bbuf[e, pl.ds(p, 512), :], NT, preferred_element_type=F32
            )
            total = jnp.sum(phi * phi, axis=0, keepdims=True)
            dens_ref[e : e + 1, p : p + 512] = total * (1.0 / BANDS)


def filtering(near, pieces, y_own, y_other, basis_values):
    anywhere = pl.BlockSpec(memory_space=pl.ANY)
    hbm = pl.BlockSpec(memory_space=pltpu.HBM)
    smem = pl.BlockSpec(memory_space=pltpu.SMEM)
    vmem = pl.BlockSpec(memory_space=pltpu.VMEM)
    return pl.pallas_call(
        filter_kernel,
        out_shape=(
            jax.ShapeDtypeStruct((4, NB, NB), BF),
            jax.ShapeDtypeStruct((4, POINTS), F32),
        ),
        in_specs=[smem, hbm, hbm] + [anywhere] * 14 + [vmem, vmem, anywhere],
        out_specs=(vmem, vmem),
        scratch_shapes=[
            pltpu.VMEM((PLANES, KDIM, WIDE), BF),
            pltpu.VMEM((2, PLANES, NB, WIDE), BF),
            pltpu.VMEM((PLANES, NB, WIDE), F32),
            pltpu.VMEM((PLANES, NB, WIDE), F32),
            pltpu.VMEM((4, POINTS, NB), BF),
            pltpu.SMEM((32,), jnp.int32),
            pltpu.SMEM((32,), jnp.int32),
            pltpu.SemaphoreType.DMA((32,)),
            pltpu.SemaphoreType.DMA,
        ],
        compiler_params=pltpu.CompilerParams(vmem_limit_bytes=38 * 2**20),
    )(near, *pieces, y_own, y_other, basis_values)


def routes(nbands):
    def index(y, h, x, lo, core):
        return (lo * 2 + core) * nbands + (y * 2 + h) * NX + x

    ny = nbands // (2 * NX)
    every = [
        (y, h, x, lo, core)
        for y in range(ny)
        for h in range(2)
        for x in range(NX)
        for lo in range(4)
        for core in range(2)
    ]

    def along_z(d):
        pairs = []
        for y, h, x, lo, core in every:
            z = (4 * h + lo + d) % 8
            pairs.append((index(y, h, x, lo, core), index(y, z // 4, x, z % 4, core)))
        return pairs

    return (
        along_z(1),
        along_z(-1),
        [(index(*q), index(q[0], q[1], q[2] ^ 1, q[3], q[4])) for q in every],
        [(index(*q), index(q[0] ^ 1, q[1], q[2], q[3], q[4])) for q in every],
        [(index(*q), index(q[0], q[1], q[2], q[3], q[4] ^ 1)) for q in every],
    )


def local(nbands, coefficients, hamiltonian, neighbours, basis_values):
    both = ("elem", "band")
    up, down, over_x, over_y, over_core = routes(nbands)
    core = lax.axis_index("elem") % 2
    pa = parity(lax.axis_index("band"))

    def move(value, pairs):
        return lax.ppermute(value, both, pairs)

    own_a, own_b = fold(hamiltonian, neighbours, pa[None])
    from_below = move(own_a, up)
    from_above = move(own_b, down)

    near = jnp.pad(neighbours.astype(BF), ((0, EDGE - 4), (0, NB - 27)))
    turned = turn(coefficients, near)
    groups = [[2 * z + c for z in range(4)] for c in range(2)]
    y_own = lax.all_to_all(turned, "elem", 0, 0, axis_index_groups=groups)
    y_other = move(y_own, over_core)

    own_swapped = [move(own_a, over_core), move(own_b, over_core)]
    from_below, y_other = lax.optimization_barrier((from_below, y_other))
    from_above, y_other, own_swapped = lax.optimization_barrier(
        (from_above, y_other, own_swapped)
    )
    far_a = move(from_below, up)
    far_b = move(from_above, down)
    below_b = move(from_below, over_x)
    below_swapped = move(from_below, over_core)
    for_y, below_swapped = lax.optimization_barrier((from_above, below_swapped))
    above_a = move(for_y, over_y)


    def table(y):
        return y[:, 4 * NB : 4 * NB + 4, :27].astype(jnp.int32)

    ids = jnp.stack([table(y_own), table(y_other)], axis=1)
    ids = jnp.where(core == 0, ids, ids[:, ::-1]).reshape(32, 27)

    ids, below_b = lax.optimization_barrier((ids, below_b))
    pieces = [own_a, own_b, from_below, from_above, far_a, far_b, below_b, above_a]
    swapped = own_swapped + [below_swapped] + [move(piece, over_core) for piece in pieces[3:]]

    filtered, partial = filtering(ids, pieces + swapped, y_own, y_other, basis_values)
    points = POINTS // nbands
    parts = partial.reshape(4, nbands, points).swapaxes(0, 1)
    parts = lax.all_to_all(parts.reshape(nbands, points // 32, 128), "band", 0, 0)
    return filtered, jnp.sum(parts, axis=0).reshape(4, points)


def solution(mesh):
    return jax.shard_map(
        functools.partial(local, mesh.shape["band"]),
        mesh=mesh,
        in_specs=(
            P("elem", None, "band"),
            P("elem", None, None, None),
            P("elem", None),
            P("elem", None, None),
        ),
        out_specs=(P("elem", None, "band"), P("elem", "band")),
        check_vma=False,
    )
```

```python
import functools

import jax
import jax.numpy as jnp
from jax import lax
from jax.experimental import pallas as pl
from jax.experimental.pallas import tpu as pltpu
from jax.sharding import PartitionSpec as P

BANDS = 8192
NB = 128
POINTS = 4096
PLANES = 8
KDIM = 12 * NB
WIDE = 4 * NB
NX = 4
EDGE = 16
BF = jnp.bfloat16
F32 = jnp.float32
NT = (((1,), (1,)), ((), ()))


def fold_kernel(pair_ref, near_ref, h0_ref, h1_ref, h2_ref, a_ref, b_ref):
    step = pl.program_id(0)
    e = lax.rem(2 * pair_ref[0] + step, 4)
    rows = lax.broadcasted_iota(jnp.int32, (NB, NB), 0)
    cols = lax.broadcasted_iota(jnp.int32, (NB, NB), 1)
    eye = (rows == cols).astype(F32).astype(BF)
    choices = ((1,), (0, 2))

    def write(out_ref):
        for dx, h_ref in enumerate((h0_ref, h1_ref, h2_ref)):
            ids = [
                near_ref[e, 9 * dx + 3 * b[0] + c[0]] for b in choices for c in choices
            ]
            spot = 0
            for b in choices:
                for c in choices:
                    total = None
                    for i in b:
                        for j in c:
                            part = h_ref[0, 3 * i + j].astype(F32)
                            total = part if total is None else total + part
                    turned = lax.dot_general(
                        eye, total.astype(BF), NT, preferred_element_type=F32
                    )
                    rank = jnp.int32(0)
                    for other in range(4):
                        if other != spot:
                            rank = rank + (ids[other] < ids[spot]).astype(jnp.int32)
                    row = pl.multiple_of((4 * dx + rank) * NB, NB)
                    out_ref[0, pl.ds(row, NB), :] = turned.astype(BF)
                    spot += 1

    @pl.when(step < 2)
    def _():
        write(a_ref)

    @pl.when(step >= 2)
    def _():
        write(b_ref)


def fold(hamiltonian, neighbours, pair):
    shape = jax.ShapeDtypeStruct((2, KDIM, NB), BF)
    return pl.pallas_call(
        fold_kernel,
        out_shape=(shape, shape),
        grid_spec=pltpu.PrefetchScalarGridSpec(
            num_scalar_prefetch=2,
            grid=(4,),
            in_specs=[
                pl.BlockSpec(
                    (1, 9, NB, NB),
                    lambda t, pair, near, dx=dx: (lax.rem(2 * pair[0] + t, 4), dx, 0, 0),
                )
                for dx in range(3)
            ],
            out_specs=(
                pl.BlockSpec((1, KDIM, NB), lambda t, pair, near: (jnp.minimum(t, 1), 0, 0)),
                pl.BlockSpec((1, KDIM, NB), lambda t, pair, near: (jnp.maximum(t - 2, 0), 0, 0)),
            ),
        ),
        compiler_params=pltpu.CompilerParams(vmem_limit_bytes=16 * 2**20),
        cost_estimate=pl.CostEstimate(
            flops=4 * 27 * 2 * NB**3, bytes_accessed=5200000, transcendentals=0
        ),
    )(pair, neighbours, hamiltonian, hamiltonian, hamiltonian)


def turn_kernel(y_ref, near_ref, out_ref):
    for e in range(4):
        block = y_ref[e].astype(F32).T.astype(BF)
        for copy in range(4):
            out_ref[copy, pl.ds(e * NB, NB), :] = block
    for copy in range(4):
        out_ref[copy, pl.ds(4 * NB, EDGE), :] = near_ref[...]


def turn(coefficients, near):
    return pl.pallas_call(
        turn_kernel,
        out_shape=jax.ShapeDtypeStruct((4, 4 * NB + EDGE, NB), BF),
        compiler_params=pltpu.CompilerParams(vmem_limit_bytes=16 * 2**20),
    )(coefficients, near)


def parity(band):
    return (band % NX + band // (2 * NX)) % 2


def piece_bases(lo, core, pa):
    pb = 1 - pa
    order = [(0, pa), (0, pb), (3, pa), (1, pb), (2, pa), (2, pb), (3, pb), (1, pa)]
    return [(((lo + z) % 4) * 2 + core) * 4 + 2 * pair for z, pair in order]


def filter_kernel(near_ref, *refs):
    h_refs = refs[:16]
    y_own, y_other, b_ref, filt_ref, dens_ref = refs[16:21]
    hbuf, ybuf, za, zb, bbuf, pid, slot, h_sems, b_sem = refs[21:]
    elem, band = lax.axis_index("elem"), lax.axis_index("band")
    lo, core = elem // 2, elem % 2
    pa = parity(band)
    bases = piece_bases(lo, core, pa) + piece_bases(lo, 1 - core, pa)

    rep = jnp.int32(0)
    for x in range(PLANES):
        ids = [near_ref[rep, 9 + 3 * b + c] for b in (1, 0) for c in (1, 0)]
        following = near_ref[rep, 18 + 4]
        for a, b in ((0, 1), (2, 3), (0, 2), (1, 3), (1, 2)):
            ids[a], ids[b] = jnp.minimum(ids[a], ids[b]), jnp.maximum(ids[a], ids[b])
        for r in range(4):
            slot[ids[r]] = 4 * x + r
        rep = following

    def place(g):
        s = slot[g]
        return s // 4, pl.multiple_of((s % 4) * NB, NB), s

    def h_copy(ref, k, g):
        x, lane, s = place(g)
        return pltpu.make_async_copy(
            ref.at[k], hbuf.at[x, :, pl.ds(lane, NB)], h_sems.at[s]
        )

    for i, ref in enumerate(h_refs):
        for k in range(2):
            h_copy(ref, k, bases[i] + k).start()

    for source, side in ((y_own, core), (y_other, 1 - core)):
        for z in range(4):
            for e in range(4):
                x, lane, _ = place((2 * z + side) * 4 + e)
                block = source[z, pl.ds(e * NB, NB), :]
                ybuf[0, x, :, pl.ds(lane, NB)] = block
                za[x, :, pl.ds(lane, NB)] = block.astype(F32)

    def around(src, x):
        return jnp.concatenate(
            [ybuf[src, (x + 7) % 8], ybuf[src, x], ybuf[src, (x + 1) % 8]], axis=1
        )

    b_copy = pltpu.make_async_copy(b_ref, bbuf, b_sem)
    for step in range(5):
        if step == 1:
            b_copy.start()
        src, dst = step % 2, 1 - step % 2
        past = zb if step % 2 == 0 else za
        for x in range(PLANES):
            if step == 0:
                for r in range(4):
                    pltpu.make_async_copy(
                        h_refs[0].at[0], hbuf.at[x, :, pl.ds(r * NB, NB)], h_sems.at[4 * x + r]
                    ).wait()
            acc = jnp.dot(around(src, x), hbuf[x], preferred_element_type=F32)
            new = acc if step == 0 else 2.0 * acc - past[x]
            past[x] = new
            ybuf[dst, x] = new.astype(BF)

    b_copy.wait()
    mine = elem * 4
    for e in range(4):
        x, lane, _ = place(mine + e)
        left = lax.rem(x + 7, 8)
        right = lax.rem(x + 1, 8)
        near = jnp.concatenate([ybuf[1, left], ybuf[1, x], ybuf[1, right]], axis=1)
        acc = jnp.dot(near, hbuf[x, :, pl.ds(lane, NB)], preferred_element_type=F32)
        last = (2.0 * acc - za[x, :, pl.ds(lane, NB)]).astype(BF)
        filt_ref[e] = last.astype(F32).T.astype(BF)
        for p in range(0, POINTS, 512):
            phi = lax.dot_general(
                last, bbuf[e, pl.ds(p, 512), :], NT, preferred_element_type=F32
            )
            total = jnp.sum(phi * phi, axis=0, keepdims=True)
            dens_ref[e : e + 1, p : p + 512] = total * (1.0 / BANDS)


def filtering(near, pieces, y_own, y_other, basis_values):
    anywhere = pl.BlockSpec(memory_space=pl.ANY)
    hbm = pl.BlockSpec(memory_space=pltpu.HBM)
    smem = pl.BlockSpec(memory_space=pltpu.SMEM)
    vmem = pl.BlockSpec(memory_space=pltpu.VMEM)
    return pl.pallas_call(
        filter_kernel,
        out_shape=(
            jax.ShapeDtypeStruct((4, NB, NB), BF),
            jax.ShapeDtypeStruct((4, POINTS), F32),
        ),
        in_specs=[smem, hbm, hbm] + [anywhere] * 14 + [vmem, vmem, anywhere],
        out_specs=(vmem, vmem),
        scratch_shapes=[
            pltpu.VMEM((PLANES, KDIM, WIDE), BF),
            pltpu.VMEM((2, PLANES, NB, WIDE), BF),
            pltpu.VMEM((PLANES, NB, WIDE), F32),
            pltpu.VMEM((PLANES, NB, WIDE), F32),
            pltpu.VMEM((4, POINTS, NB), BF),
            pltpu.SMEM((32,), jnp.int32),
            pltpu.SMEM((32,), jnp.int32),
            pltpu.SemaphoreType.DMA((32,)),
            pltpu.SemaphoreType.DMA,
        ],
        compiler_params=pltpu.CompilerParams(vmem_limit_bytes=38 * 2**20),
    )(near, *pieces, y_own, y_other, basis_values)


def routes(nbands):
    def index(y, h, x, lo, core):
        return (lo * 2 + core) * nbands + (y * 2 + h) * NX + x

    ny = nbands // (2 * NX)
    every = [
        (y, h, x, lo, core)
        for y in range(ny)
        for h in range(2)
        for x in range(NX)
        for lo in range(4)
        for core in range(2)
    ]

    def along_z(d):
        pairs = []
        for y, h, x, lo, core in every:
            z = (4 * h + lo + d) % 8
            pairs.append((index(y, h, x, lo, core), index(y, z // 4, x, z % 4, core)))
        return pairs

    return (
        along_z(1),
        along_z(-1),
        [(index(*q), index(q[0], q[1], q[2] ^ 1, q[3], q[4])) for q in every],
        [(index(*q), index(q[0] ^ 1, q[1], q[2], q[3], q[4])) for q in every],
        [(index(*q), index(q[0], q[1], q[2], q[3], q[4] ^ 1)) for q in every],
    )


def local(nbands, coefficients, hamiltonian, neighbours, basis_values):
    both = ("elem", "band")
    up, down, over_x, over_y, over_core = routes(nbands)
    core = lax.axis_index("elem") % 2
    pa = parity(lax.axis_index("band"))

    def move(value, pairs):
        return lax.ppermute(value, both, pairs)

    own_a, own_b = fold(hamiltonian, neighbours, pa[None])
    from_below = move(own_a, up)
    from_above = move(own_b, down)

    near = jnp.pad(neighbours.astype(BF), ((0, EDGE - 4), (0, NB - 27)))
    turned = turn(coefficients, near)
    groups = [[2 * z + c for z in range(4)] for c in range(2)]
    y_own = lax.all_to_all(turned, "elem", 0, 0, axis_index_groups=groups)
    y_other = move(y_own, over_core)

    own_swapped = [move(own_a, over_core), move(own_b, over_core)]
    from_below, y_other = lax.optimization_barrier((from_below, y_other))
    from_above, y_other = lax.optimization_barrier((from_above, y_other))
    far_a = move(from_below, up)
    far_b = move(from_above, down)
    below_b = move(from_below, over_x)
    below_swapped = move(from_below, over_core)
    for_y, below_swapped, own_swapped = lax.optimization_barrier(
        (from_above, below_swapped, own_swapped)
    )
    above_a = move(for_y, over_y)


    def table(y):
        return y[:, 4 * NB : 4 * NB + 4, :27].astype(jnp.int32)

    ids = jnp.stack([table(y_own), table(y_other)], axis=1)
    ids = jnp.where(core == 0, ids, ids[:, ::-1]).reshape(32, 27)

    ids, below_b = lax.optimization_barrier((ids, below_b))
    pieces = [own_a, own_b, from_below, from_above, far_a, far_b, below_b, above_a]
    swapped = own_swapped + [below_swapped] + [move(piece, over_core) for piece in pieces[3:]]

    filtered, partial = filtering(ids, pieces + swapped, y_own, y_other, basis_values)
    points = POINTS // nbands
    parts = partial.reshape(4, nbands, points).swapaxes(0, 1)
    parts = lax.all_to_all(parts.reshape(nbands, points // 32, 128), "band", 0, 0)
    return filtered, jnp.sum(parts, axis=0).reshape(4, points)


def solution(mesh):
    return jax.shard_map(
        functools.partial(local, mesh.shape["band"]),
        mesh=mesh,
        in_specs=(
            P("elem", None, "band"),
            P("elem", None, None, None),
            P("elem", None),
            P("elem", None, None),
        ),
        out_specs=(P("elem", None, "band"), P("elem", "band")),
        check_vma=False,
    )
```

```python
import functools

import jax
import jax.numpy as jnp
from jax import lax
from jax.experimental import pallas as pl
from jax.experimental.pallas import tpu as pltpu
from jax.sharding import PartitionSpec as P

BANDS = 8192
NB = 128
POINTS = 4096
PLANES = 8
KDIM = 12 * NB
WIDE = 4 * NB
NX = 4
EDGE = 16
BF = jnp.bfloat16
F32 = jnp.float32
NT = (((1,), (1,)), ((), ()))


def fold_kernel(pair_ref, near_ref, h0_ref, h1_ref, h2_ref, a_ref, b_ref):
    step = pl.program_id(0)
    e = lax.rem(2 * pair_ref[0] + step, 4)
    rows = lax.broadcasted_iota(jnp.int32, (NB, NB), 0)
    cols = lax.broadcasted_iota(jnp.int32, (NB, NB), 1)
    eye = (rows == cols).astype(F32).astype(BF)
    choices = ((1,), (0, 2))

    def write(out_ref):
        for dx, h_ref in enumerate((h0_ref, h1_ref, h2_ref)):
            ids = [
                near_ref[e, 9 * dx + 3 * b[0] + c[0]] for b in choices for c in choices
            ]
            spot = 0
            for b in choices:
                for c in choices:
                    total = None
                    for i in b:
                        for j in c:
                            part = h_ref[0, 3 * i + j].astype(F32)
                            total = part if total is None else total + part
                    turned = lax.dot_general(
                        eye, total.astype(BF), NT, preferred_element_type=F32
                    )
                    rank = jnp.int32(0)
                    for other in range(4):
                        if other != spot:
                            rank = rank + (ids[other] < ids[spot]).astype(jnp.int32)
                    row = pl.multiple_of((4 * dx + rank) * NB, NB)
                    out_ref[0, pl.ds(row, NB), :] = turned.astype(BF)
                    spot += 1

    @pl.when(step < 2)
    def _():
        write(a_ref)

    @pl.when(step >= 2)
    def _():
        write(b_ref)


def fold(hamiltonian, neighbours, pair):
    shape = jax.ShapeDtypeStruct((2, KDIM, NB), BF)
    return pl.pallas_call(
        fold_kernel,
        out_shape=(shape, shape),
        grid_spec=pltpu.PrefetchScalarGridSpec(
            num_scalar_prefetch=2,
            grid=(4,),
            in_specs=[
                pl.BlockSpec(
                    (1, 9, NB, NB),
                    lambda t, pair, near, dx=dx: (lax.rem(2 * pair[0] + t, 4), dx, 0, 0),
                )
                for dx in range(3)
            ],
            out_specs=(
                pl.BlockSpec((1, KDIM, NB), lambda t, pair, near: (jnp.minimum(t, 1), 0, 0)),
                pl.BlockSpec((1, KDIM, NB), lambda t, pair, near: (jnp.maximum(t - 2, 0), 0, 0)),
            ),
        ),
        compiler_params=pltpu.CompilerParams(vmem_limit_bytes=16 * 2**20),
        cost_estimate=pl.CostEstimate(
            flops=4 * 27 * 2 * NB**3, bytes_accessed=5200000, transcendentals=0
        ),
    )(pair, neighbours, hamiltonian, hamiltonian, hamiltonian)


def turn_kernel(y_ref, near_ref, out_ref):
    for e in range(4):
        block = y_ref[e].astype(F32).T.astype(BF)
        for copy in range(4):
            out_ref[copy, pl.ds(e * NB, NB), :] = block
    for copy in range(4):
        out_ref[copy, pl.ds(4 * NB, EDGE), :] = near_ref[...]


def turn(coefficients, near):
    return pl.pallas_call(
        turn_kernel,
        out_shape=jax.ShapeDtypeStruct((4, 4 * NB + EDGE, NB), BF),
        compiler_params=pltpu.CompilerParams(vmem_limit_bytes=16 * 2**20),
    )(coefficients, near)


def parity(band):
    return (band % NX + band // (2 * NX)) % 2


def piece_bases(lo, core, pa):
    pb = 1 - pa
    order = [(0, pa), (0, pb), (3, pa), (1, pb), (2, pa), (2, pb), (3, pb), (1, pa)]
    return [(((lo + z) % 4) * 2 + core) * 4 + 2 * pair for z, pair in order]


def filter_kernel(near_ref, *refs):
    h_refs = refs[:16]
    y_own, y_other, b_ref, filt_ref, dens_ref = refs[16:21]
    hbuf, ybuf, za, zb, bbuf, pid, slot, h_sems, b_sem = refs[21:]
    elem, band = lax.axis_index("elem"), lax.axis_index("band")
    lo, core = elem // 2, elem % 2
    pa = parity(band)
    bases = piece_bases(lo, core, pa) + piece_bases(lo, 1 - core, pa)

    rep = jnp.int32(0)
    for x in range(PLANES):
        ids = [near_ref[rep, 9 + 3 * b + c] for b in (1, 0) for c in (1, 0)]
        following = near_ref[rep, 18 + 4]
        for a, b in ((0, 1), (2, 3), (0, 2), (1, 3), (1, 2)):
            ids[a], ids[b] = jnp.minimum(ids[a], ids[b]), jnp.maximum(ids[a], ids[b])
        for r in range(4):
            slot[ids[r]] = 4 * x + r
        rep = following

    def place(g):
        s = slot[g]
        return s // 4, pl.multiple_of((s % 4) * NB, NB), s

    for dx in range(3):
        share = pl.ds(dx * WIDE, WIDE)
        for i, ref in enumerate(h_refs):
            for k in range(2):
                x, lane, s = place(bases[i] + k)
                pltpu.make_async_copy(
                    ref.at[k, share], hbuf.at[x, share, pl.ds(lane, NB)], h_sems.at[dx, s]
                ).start()

    for source, side in ((y_own, core), (y_other, 1 - core)):
        for z in range(4):
            for e in range(4):
                x, lane, _ = place((2 * z + side) * 4 + e)
                block = source[z, pl.ds(e * NB, NB), :]
                ybuf[0, x, :, pl.ds(lane, NB)] = block
                za[x, :, pl.ds(lane, NB)] = block.astype(F32)

    def around(src, x):
        return jnp.concatenate(
            [ybuf[src, (x + 7) % 8], ybuf[src, x], ybuf[src, (x + 1) % 8]], axis=1
        )

    for dx in range(3):
        share = pl.ds(dx * WIDE, WIDE)
        for x in range(PLANES):
            for r in range(4):
                pltpu.make_async_copy(
                    h_refs[0].at[0, share],
                    hbuf.at[x, share, pl.ds(r * NB, NB)],
                    h_sems.at[dx, 4 * x + r],
                ).wait()
            part = jnp.dot(
                ybuf[0, (x + dx + 7) % 8],
                hbuf[x, dx * WIDE : (dx + 1) * WIDE],
                preferred_element_type=F32,
            )
            new = part if dx == 0 else zb[x] + part
            zb[x] = new
            if dx == 2:
                ybuf[1, x] = new.astype(BF)

    b_copy = pltpu.make_async_copy(b_ref, bbuf, b_sem)
    for step in range(1, 5):
        if step == 1:
            b_copy.start()
        src, dst = step % 2, 1 - step % 2
        past = zb if step % 2 == 0 else za
        for x in range(PLANES):
            acc = jnp.dot(around(src, x), hbuf[x], preferred_element_type=F32)
            new = 2.0 * acc - past[x]
            past[x] = new
            ybuf[dst, x] = new.astype(BF)

    b_copy.wait()
    mine = elem * 4
    for e in range(4):
        x, lane, _ = place(mine + e)
        left = lax.rem(x + 7, 8)
        right = lax.rem(x + 1, 8)
        near = jnp.concatenate([ybuf[1, left], ybuf[1, x], ybuf[1, right]], axis=1)
        acc = jnp.dot(near, hbuf[x, :, pl.ds(lane, NB)], preferred_element_type=F32)
        last = (2.0 * acc - za[x, :, pl.ds(lane, NB)]).astype(BF)
        filt_ref[e] = last.astype(F32).T.astype(BF)
        for p in range(0, POINTS, 512):
            phi = lax.dot_general(
                last, bbuf[e, pl.ds(p, 512), :], NT, preferred_element_type=F32
            )
            total = jnp.sum(phi * phi, axis=0, keepdims=True)
            dens_ref[e : e + 1, p : p + 512] = total * (1.0 / BANDS)


def filtering(near, pieces, y_own, y_other, basis_values):
    anywhere = pl.BlockSpec(memory_space=pl.ANY)
    hbm = pl.BlockSpec(memory_space=pltpu.HBM)
    smem = pl.BlockSpec(memory_space=pltpu.SMEM)
    vmem = pl.BlockSpec(memory_space=pltpu.VMEM)
    return pl.pallas_call(
        filter_kernel,
        out_shape=(
            jax.ShapeDtypeStruct((4, NB, NB), BF),
            jax.ShapeDtypeStruct((4, POINTS), F32),
        ),
        in_specs=[smem, hbm, hbm] + [anywhere] * 14 + [vmem, vmem, anywhere],
        out_specs=(vmem, vmem),
        scratch_shapes=[
            pltpu.VMEM((PLANES, KDIM, WIDE), BF),
            pltpu.VMEM((2, PLANES, NB, WIDE), BF),
            pltpu.VMEM((PLANES, NB, WIDE), F32),
            pltpu.VMEM((PLANES, NB, WIDE), F32),
            pltpu.VMEM((4, POINTS, NB), BF),
            pltpu.SMEM((32,), jnp.int32),
            pltpu.SMEM((32,), jnp.int32),
            pltpu.SemaphoreType.DMA((3, 32)),
            pltpu.SemaphoreType.DMA,
        ],
        compiler_params=pltpu.CompilerParams(vmem_limit_bytes=38 * 2**20),
    )(near, *pieces, y_own, y_other, basis_values)


def routes(nbands):
    def index(y, h, x, lo, core):
        return (lo * 2 + core) * nbands + (y * 2 + h) * NX + x

    ny = nbands // (2 * NX)
    every = [
        (y, h, x, lo, core)
        for y in range(ny)
        for h in range(2)
        for x in range(NX)
        for lo in range(4)
        for core in range(2)
    ]

    def along_z(d):
        pairs = []
        for y, h, x, lo, core in every:
            z = (4 * h + lo + d) % 8
            pairs.append((index(y, h, x, lo, core), index(y, z // 4, x, z % 4, core)))
        return pairs

    return (
        along_z(1),
        along_z(-1),
        [(index(*q), index(q[0], q[1], q[2] ^ 1, q[3], q[4])) for q in every],
        [(index(*q), index(q[0] ^ 1, q[1], q[2], q[3], q[4])) for q in every],
        [(index(*q), index(q[0], q[1], q[2], q[3], q[4] ^ 1)) for q in every],
    )


def local(nbands, coefficients, hamiltonian, neighbours, basis_values):
    both = ("elem", "band")
    up, down, over_x, over_y, over_core = routes(nbands)
    core = lax.axis_index("elem") % 2
    pa = parity(lax.axis_index("band"))

    def move(value, pairs):
        return lax.ppermute(value, both, pairs)

    own_a, own_b = fold(hamiltonian, neighbours, pa[None])
    from_below = move(own_a, up)
    from_above = move(own_b, down)

    near = jnp.pad(neighbours.astype(BF), ((0, EDGE - 4), (0, NB - 27)))
    turned = turn(coefficients, near)
    groups = [[2 * z + c for z in range(4)] for c in range(2)]
    y_own = lax.all_to_all(turned, "elem", 0, 0, axis_index_groups=groups)
    y_other = move(y_own, over_core)

    own_swapped = [move(own_a, over_core), move(own_b, over_core)]
    from_above, y_other, own_swapped = lax.optimization_barrier(
        (from_above, y_other, own_swapped)
    )
    far_a = move(from_below, up)
    far_b = move(from_above, down)
    below_b = move(from_below, over_x)
    above_a = move(from_above, over_y)


    def table(y):
        return y[:, 4 * NB : 4 * NB + 4, :27].astype(jnp.int32)

    ids = jnp.stack([table(y_own), table(y_other)], axis=1)
    ids = jnp.where(core == 0, ids, ids[:, ::-1]).reshape(32, 27)

    ids, below_b = lax.optimization_barrier((ids, below_b))
    pieces = [own_a, own_b, from_below, from_above, far_a, far_b, below_b, above_a]
    swapped = own_swapped + [move(piece, over_core) for piece in pieces[2:]]

    filtered, partial = filtering(ids, pieces + swapped, y_own, y_other, basis_values)
    points = POINTS // nbands
    parts = partial.reshape(4, nbands, points).swapaxes(0, 1)
    parts = lax.all_to_all(parts.reshape(nbands, points // 32, 128), "band", 0, 0)
    return filtered, jnp.sum(parts, axis=0).reshape(4, points)


def solution(mesh):
    return jax.shard_map(
        functools.partial(local, mesh.shape["band"]),
        mesh=mesh,
        in_specs=(
            P("elem", None, "band"),
            P("elem", None, None, None),
            P("elem", None),
            P("elem", None, None),
        ),
        out_specs=(P("elem", None, "band"), P("elem", "band")),
        check_vma=False,
    )
```
